128 devices in a mesh: ctx: 16 (over x, y_hi, core), exp: 8 (over y_lo, z).
Axes of the slice: x: 4, y: 4 (y_hi: 2, y_lo: 2; y = y_hi * 2 + y_lo), z: 4, core: 2. Of those that a mesh axis runs over, the one named last changes fastest.
Arguments:
- hidden_in: bfloat16 [2048, 4096], P('ctx'), may hold values from -6 to 6
- attn_gain: bfloat16 [4096], replicated, may hold values from 0.099609375 to 1.8984375
- w_query: bfloat16 [4096, 4096], P('ctx', 'exp'), may hold values from -0.1875 to 0.1875
- w_key: bfloat16 [4096, 1024], P('ctx', 'exp'), may hold values from -0.09375 to 0.09375
- w_value: bfloat16 [4096, 1024], P('ctx', 'exp'), may hold values from -0.09375 to 0.09375
- w_out: bfloat16 [4096, 4096], P('exp', 'ctx'), may hold values from -0.375 to 0.375
- prior_keys: bfloat16 [2048, 1024], P('ctx', 'exp'), may hold values from -100 to 100
- prior_values: bfloat16 [2048, 1024], P('ctx', 'exp'), may hold values from -6 to 6
- stretch_offset: int32 [1], replicated, may hold values from 2048 to 30720
- ffn_gain: bfloat16 [4096], replicated, may hold values from 0.099609375 to 1.8984375
- w_gate: bfloat16 [8, 4096, 14336], P('exp', None, 'ctx'), may hold values from -0.09375 to 0.09375
- w_up: bfloat16 [8, 4096, 14336], P('exp', None, 'ctx'), may hold values from -0.09375 to 0.09375
- w_down: bfloat16 [8, 14336, 4096], P('exp', 'ctx'), may hold values from -0.15625 to 0.15625
- expert_ids: int32 [2048, 2], replicated, may hold values from 0 to 7, all different within a row; in each aligned block of 16 rows (0 to 15, 16 to 31, ...) at most 8 rows name the same one
- gate_weights: float32 [2048, 2], P(('ctx', 'exp')), may hold values from 0.1 to 0.9
Outputs:
- output: bfloat16 [2048, 4096], P(('ctx', 'exp'))
The draws below stay inside these ranges and needn't reach their ends.
Inputs may be any that keep to these rules, and one draw needn't show every extreme that they name: `expert_ids`: each row names two different experts. Within each aligned block of 16 rows no expert is named by more than 8 rows, and in some blocks one expert is named by exactly 8. prior_keys and prior_values belong to positions stretch_offset - 2048 to stretch_offset - 1, in order; prior_keys are already rotated at those positions.
All inputs are finite; a program needn't handle non-finite values.
Results may differ from the reference program's by a relative error of at most 0.03.
The reference program's roundings to bfloat16 on the way count: a program that leaves them out, or rounds other values in their place, can miss the bound.
Values may be sent and summed in bfloat16 or wider, within the bound.
A program may use at most 128 MiB of HBM per device.

```python
import math
import jax
import jax.numpy as jnp
import numpy as np
from jax import lax

D = 4096
HEADS = 32
KV_HEADS = 8
HEAD_DIM = 128
FF = 14336
EXPERTS = 8
STRETCH = 2048
WINDOW_SPAN = 2048
TOK_DEV = 16
CAP = 8
N_CTX = 16
N_EXP = 8


def draw_prior_keys(key, part):
    key = jax.random.fold_in(key, 11)
    key_one = jax.random.fold_in(key, 0)
    full_shape = (WINDOW_SPAN, KV_HEADS * HEAD_DIM)
    table_entries = jnp.clip(jax.random.normal(key_one, full_shape, jnp.float32), -6.0, 6.0)
    return table_entries.astype(jnp.bfloat16)


def level_of(key, extent, cuts, smallest, top_value):
    def one(position, parts):
        heights = jax.random.uniform(jax.random.fold_in(jax.random.fold_in(key, 6), position), (parts,), jnp.float32, smallest / len(cuts), top_value / len(cuts))
        return jnp.repeat(jnp.exp(heights), extent[position] // parts).reshape((-1,) + (1,) * (len(extent) - position - 1))

    gain = one(*cuts[0])
    for cut in cuts[1:]:
        gain = gain * one(*cut)
    return gain


def deal_out(own_key, own, number, rows, amount, top, limit, lean):
    order = jax.random.permutation(own_key, amount)
    packed, usual = shares(amount, rows * top, limit, lean, True), shares(amount, rows * top, limit, lean, False)
    places = jnp.arange(amount)

    def named(sizes, turn):
        used = int((sizes > 0).sum())
        fixed = max(1, used // 4)
        moved = fixed + (places - fixed + turn * (used - fixed)) % max(1, amount - fixed)
        return jnp.zeros((amount,), jnp.int32).at[order[jnp.where(places < fixed, places, moved)]].set(jnp.asarray(sizes, jnp.int32))

    sizes = jnp.where(number % 4 == 0, named(packed, number // 4), named(usual, number - number // 4 - 1))
    mixed = jax.random.permutation(jax.random.fold_in(own, 3), amount)
    donor, receiver = mixed[0:amount // 2 * 2:2], mixed[1:amount // 2 * 2:2]
    slack = jnp.minimum(sizes[donor] - 1, limit - sizes[receiver]) // 2
    slack = jnp.where((donor == order[0]) | (receiver == order[0]) | (sizes[receiver] == 0), 0, jnp.maximum(slack, 0))
    moved = jax.random.randint(jax.random.fold_in(own, 4), (amount // 2,), 0, 1 << 20) % (slack + 1)
    sizes = sizes.at[donor].add(-moved).at[receiver].add(moved)
    labels = jnp.searchsorted(jnp.cumsum(sizes), jnp.arange(rows * top), side="right").astype(jnp.int32)
    grid = labels.reshape(top, rows).T
    grid = grid[jax.random.permutation(jax.random.fold_in(own, 1), rows)]
    turn = jax.random.randint(jax.random.fold_in(own, 2), (rows, 1), 0, top)
    return jnp.take_along_axis(grid, (jnp.arange(top)[None, :] + turn) % top, axis=1)


def shares(count, total, most, slope, full):
    loads = [(1 << 20) // math.isqrt(rank ** slope) + 1 for rank in range(1, count + 1)]
    largest = most if full else min(most, max(-(-total // count), total * loads[0] // sum(loads)))
    least = 1 if total - largest >= count - 1 else 0
    holding, rest = [largest] + [least] * (count - 1), total - largest - least * (count - 1)
    while rest > 0:
        free = [i for i in range(1, count) if holding[i] < largest] or [i for i in range(1, count) if holding[i] < most]
        mass, remaining = sum([loads[i] for i in free]), rest
        for i in free:
            extra = min(most - holding[i], max(1, remaining * loads[i] // mass), rest)
            holding[i] = holding[i] + extra
            rest = rest - extra
    return np.array(holding)


def gaussian(key, shape, scale, limit, pieces=(), kind=jnp.bfloat16):
    gain = level_of(key, shape, pieces, -0.22, 0.18) if pieces else 1.0
    array = jax.random.normal(key, shape, jnp.float32) * scale * gain
    return jnp.minimum(jnp.maximum(array, -limit), limit).astype(kind)


def setup_inputs(seed: int = 0) -> dict:
    splits = jax.random.split(jax.random.key(seed), 16)
    hidden_in = gaussian(splits[0], (STRETCH, D), 1.0, 6.0, ((0, 16),))
    attn_gain = jnp.clip(1.0 + 0.18 * jax.random.normal(splits[1], (D,), jnp.float32), 0.099609375, 1.8984375).astype(jnp.bfloat16)
    w_query = gaussian(splits[2], (D, HEADS * HEAD_DIM), (D // 4) ** -0.5, 0.1875, ((0, 16), (1, 8)))
    w_key = gaussian(splits[3], (D, KV_HEADS * HEAD_DIM), D ** -0.5, 0.09375, ((0, 16), (1, 8)))
    w_value = gaussian(splits[4], (D, KV_HEADS * HEAD_DIM), D ** -0.5, 0.09375, ((0, 16), (1, 8)))
    w_out = gaussian(splits[5], (HEADS * HEAD_DIM, D), (HEADS * HEAD_DIM // 16) ** -0.5, 0.375, ((0, 8), (1, 16)))
    prior_keys = draw_prior_keys(jax.random.fold_in(splits[15], 71), 0)
    prior_values = gaussian(splits[7], (WINDOW_SPAN, KV_HEADS * HEAD_DIM), 1.0, 6.0, ((0, 16), (1, 8)))
    stretch_offset = jax.random.randint(splits[8], (1,), WINDOW_SPAN, 32769 - STRETCH).astype(jnp.int32)
    ffn_gain = jnp.clip(1.0 + 0.18 * jax.random.normal(splits[9], (D,), jnp.float32), 0.099609375, 1.8984375).astype(jnp.bfloat16)
    w_gate = gaussian(splits[10], (EXPERTS, D, FF), D ** -0.5, 0.09375, ((0, 8), (2, 16)))
    w_up = gaussian(splits[11], (EXPERTS, D, FF), D ** -0.5, 0.09375, ((0, 8), (2, 16)))
    w_down = gaussian(splits[12], (EXPERTS, FF, D), (FF // 9) ** -0.5, 0.15625, ((0, 8), (1, 16)))
    expert_ids_keys = jax.random.split(jax.random.fold_in(splits[13], 1), STRETCH // TOK_DEV)
    expert_ids_turns = jax.random.permutation(jax.random.fold_in(splits[13], 3), STRETCH // TOK_DEV)
    expert_ids = jax.vmap(lambda own, number: deal_out(jax.random.fold_in(splits[13], 2), own, number, TOK_DEV, EXPERTS, 2, CAP, 2))(expert_ids_keys, expert_ids_turns).reshape((STRETCH, 2))
    gate_weights = jnp.clip(0.1 + 0.79999997 * jax.random.uniform(splits[14], (STRETCH, 2), jnp.float32) ** level_of(splits[14], (STRETCH, 2), ((0, 128),), -0.2, 0.2), 0.1, 0.9)
    return dict(hidden_in=hidden_in, attn_gain=attn_gain, w_query=w_query, w_key=w_key, w_value=w_value, w_out=w_out, prior_keys=prior_keys, prior_values=prior_values, stretch_offset=stretch_offset, ffn_gain=ffn_gain, w_gate=w_gate, w_up=w_up, w_down=w_down, expert_ids=expert_ids, gate_weights=gate_weights)


def rms_scale(matrix, gain_vec):
    widened = matrix.astype(jnp.float32)
    inverse = lax.rsqrt(lax.optimization_barrier(jnp.mean(widened * widened, axis=-1, keepdims=True)) + 1e-05)
    return (widened * inverse * gain_vec.astype(jnp.float32)).astype(jnp.bfloat16)

def rotate(matrix, positions, head_dim):
    row_count = matrix.shape[0]
    head_count = matrix.shape[1] // head_dim
    half_dim = head_dim // 2
    shaped = matrix.reshape(row_count, head_count, head_dim)
    frequency = jnp.exp(jnp.arange(half_dim).astype(jnp.float32) * (-2.0 * math.log(1000000.0) / head_dim))
    angles = positions.astype(jnp.float32)[:, None] * frequency[None, :]
    cosine = jnp.cos(angles)[:, None, :]
    sine_part = jnp.sin(angles)[:, None, :]
    first_half = shaped[:, :, :half_dim]
    second_half = shaped[:, :, half_dim:]
    turned = jnp.concatenate([first_half * cosine - second_half * sine_part, second_half * cosine + first_half * sine_part], axis=2)
    return turned.reshape(row_count, head_count * head_dim)

def reference(hidden_in, attn_gain, w_query, w_key, w_value, w_out, prior_keys, prior_values, stretch_offset, ffn_gain, w_gate, w_up, w_down, expert_ids, gate_weights):
    segment_length = hidden_in.shape[0]
    model_width = hidden_in.shape[1]
    head_group = HEADS // KV_HEADS
    normed = rms_scale(hidden_in, attn_gain)
    positions = stretch_offset[0] + jnp.arange(segment_length, dtype=jnp.int32)
    query_rot = rotate(jnp.dot(normed, w_query, preferred_element_type=jnp.float32), positions, HEAD_DIM).astype(jnp.bfloat16)
    key_now = rotate(jnp.dot(normed, w_key, preferred_element_type=jnp.float32), positions, HEAD_DIM).astype(jnp.bfloat16)
    value_now = jnp.dot(normed, w_value, preferred_element_type=jnp.float32).astype(jnp.bfloat16)
    all_keys = jnp.concatenate([prior_keys, key_now], axis=0)
    all_values = jnp.concatenate([prior_values, value_now], axis=0)
    token_pos = jnp.arange(segment_length, dtype=jnp.int32)
    visible = jnp.concatenate([token_pos[None, :] > token_pos[:, None], token_pos[None, :] <= token_pos[:, None]], axis=1)

    def one_head(kv_head):
        head_keys = lax.dynamic_slice_in_dim(all_keys, kv_head * HEAD_DIM, HEAD_DIM, 1).astype(jnp.float32)
        head_values = lax.dynamic_slice_in_dim(all_values, kv_head * HEAD_DIM, HEAD_DIM, 1).astype(jnp.float32)
        queries = lax.dynamic_slice_in_dim(query_rot, kv_head * head_group * HEAD_DIM, head_group * HEAD_DIM, 1)
        queries = queries.reshape(segment_length, head_group, HEAD_DIM).astype(jnp.float32)
        scores = jnp.einsum('tgd,kd->gtk', queries, head_keys) / math.sqrt(HEAD_DIM)
        scores = jnp.where(visible[None], scores, -1e+30)
        row_best = lax.optimization_barrier(jnp.max(scores, axis=2, keepdims=True))
        weights = jnp.where(visible[None], jnp.exp(scores - row_best), 0.0)
        row_mass = lax.optimization_barrier(jnp.sum(weights, axis=2, keepdims=True))
        probs = lax.optimization_barrier(weights.astype(jnp.bfloat16)).astype(jnp.float32)
        blended = jnp.einsum('gtk,kd->gtd', probs, head_values) / row_mass
        return blended.astype(jnp.bfloat16)
    head_outputs = lax.map(one_head, jnp.arange(KV_HEADS, dtype=jnp.int32))
    attended = head_outputs.transpose(2, 0, 1, 3).reshape(segment_length, HEADS * HEAD_DIM)
    mixed_out = jnp.dot(attended, w_out, preferred_element_type=jnp.float32)
    residual = (hidden_in.astype(jnp.float32) + mixed_out).astype(jnp.bfloat16)
    normed_ffn = rms_scale(residual, ffn_gain)
    most_rows = min(segment_length, N_CTX * N_EXP * CAP)

    def expert_step(running, inputs):
        gate_mat, up_mat, down_mat, expert_index = inputs
        matches = expert_ids == expert_index
        weight_of = lax.optimization_barrier(jnp.sum(jnp.where(matches, gate_weights, 0.0), axis=1))
        hit_rows = jnp.any(matches, axis=1)
        ordering = jnp.argsort(jnp.where(hit_rows, 0, 1).astype(jnp.int32) * segment_length + jnp.arange(segment_length, dtype=jnp.int32))
        picked = ordering[:most_rows]
        rows_in = normed_ffn[picked]
        gate_part = jnp.dot(rows_in, gate_mat, preferred_element_type=jnp.float32)
        up_part = jnp.dot(rows_in, up_mat, preferred_element_type=jnp.float32)
        hidden_act = (jax.nn.silu(gate_part) * up_part).astype(jnp.bfloat16)
        expert_out = jnp.dot(hidden_act, down_mat, preferred_element_type=jnp.float32).astype(jnp.bfloat16)
        scaled = weight_of[picked][:, None] * expert_out.astype(jnp.float32)
        return (running.at[picked].add(scaled), None)
    running, _ = lax.scan(expert_step, jnp.zeros((segment_length, model_width), jnp.float32), (w_gate, w_up, w_down, jnp.arange(EXPERTS, dtype=jnp.int32)))
    return (residual.astype(jnp.float32) + running).astype(jnp.bfloat16)
```

```python
import functools
import math

import jax
import jax.numpy as jnp
from jax import lax
from jax.experimental import pallas as pl
from jax.experimental.pallas import tpu as pltpu
from jax.sharding import PartitionSpec as P

HEADS = 32
KV_HEADS = 8
HEAD_DIM = 128
MESH = pl.DeviceIdType.MESH
NX, NY, NK = 4, 2, 2

Y_THEN_X = (
    (None, (0, 0, 0), None, "Y"),
    (None, (0, 0, 0), None, "R"),
    (None, (0, 0, 0), None, "L"),
    (None, (0, 0, 0), None, "S"),
    (0, (0, 1, 0), None, "R"),
    (0, (0, 1, 0), None, "L"),
    (0, (0, 1, 0), None, "S"),
    (1, (-1, 0, 0), 0, "R"),
    (1, (-1, 0, 0), None, "S"),
    (2, (1, 0, 0), 1, "L"),
    (2, (1, 0, 0), None, "S"),
    (4, (-1, 1, 0), 0, "R"),
    (4, (-1, 1, 0), None, "S"),
    (5, (1, 1, 0), 1, "L"),
    (5, (1, 1, 0), None, "S"),
    (7, (2, 0, 0), 0, "S"),
    (9, (2, 0, 0), 1, "S"),
    (11, (2, 1, 0), 0, "S"),
    (13, (2, 1, 0), 1, "S"),
)
X_THEN_Y = (
    (None, (0, 0, 0), None, "R"),
    (None, (0, 0, 0), None, "L"),
    (None, (0, 0, 0), None, "Y"),
    (None, (0, 0, 0), None, "S"),
    (0, (-1, 0, 0), 0, "R"),
    (0, (-1, 0, 0), None, "Y"),
    (0, (-1, 0, 0), None, "S"),
    (1, (1, 0, 0), 1, "L"),
    (1, (1, 0, 0), None, "Y"),
    (1, (1, 0, 0), None, "S"),
    (2, (0, 1, 0), None, "S"),
    (4, (2, 0, 0), 0, "Y"),
    (4, (2, 0, 0), 0, "S"),
    (7, (2, 0, 0), 1, "Y"),
    (7, (2, 0, 0), 1, "S"),
    (5, (-1, 1, 0), None, "S"),
    (8, (1, 1, 0), None, "S"),
    (11, (2, 1, 0), 0, "S"),
    (13, (2, 1, 0), 1, "S"),
)
N_TRANSFERS = 19
STEP = {"R": (1, 0, 0), "L": (-1, 0, 0), "Y": (0, 1, 0), "S": (0, 0, 1)}
FROM = {"R": (-1, 0, 0), "L": (1, 0, 0), "Y": (0, 1, 0), "S": (0, 0, 1)}


def ctx_at(delta):
    c = lax.axis_index("ctx")
    x = (c // 4 + delta[0] + NX) % NX
    y = ((c // 2) % 2 + delta[1]) % NY
    k = (c % 2 + delta[2]) % NK
    return x * 4 + y * 2 + k


def plus(a, b):
    return ((a[0] + b[0]) % NX, (a[1] + b[1]) % NY, (a[2] + b[2]) % NK)


def greet(targets):
    barrier = pltpu.get_barrier_semaphore()
    for target in targets:
        pl.semaphore_signal(barrier, inc=1, device_id=target, device_id_type=MESH)
    pl.semaphore_wait(barrier, len(targets))


def ctx_neighbours():
    e = lax.axis_index("exp")
    return [(ctx_at(STEP[t]), e) for t in "RLYS"]


class Gather:
    def __init__(self, number, mode, own, slot, send, recv):
        self.number, self.mode, self.own, self.slot = number, mode, own, slot
        self.send, self.recv = send, recv
        self.depth = []
        for trigger, _, _, _ in mode:
            self.depth.append(0 if trigger is None else self.depth[trigger] + 1)

    def copy(self, j, arriving):
        trigger, rel, half, to = self.mode[j]
        e = lax.axis_index("exp")
        at = plus(FROM[to], rel) if arriving else rel
        ref = self.slot(ctx_at(at), half)
        source = self.own if trigger is None and not arriving else ref
        return pltpu.make_async_remote_copy(
            src_ref=source,
            dst_ref=ref,
            send_sem=self.send.at[self.number, j],
            recv_sem=self.recv.at[self.number, j],
            device_id=(ctx_at(STEP[to]), e),
            device_id_type=MESH,
        )

    def start(self, trigger):
        for j, transfer in enumerate(self.mode):
            if transfer[0] == trigger:
                self.copy(j, False).start()

    def arrive(self, j):
        self.copy(j, True).wait_recv()

    def events(self):
        triggers = sorted({t[0] for t in self.mode if t[0] is not None})
        out = [(0, functools.partial(self.start, None))]

        def forward(j):
            self.arrive(j)
            self.start(j)

        for j in triggers:
            out.append((self.depth[j] + 1, functools.partial(forward, j)))
        return out

    def finish(self):
        forwarded = {t[0] for t in self.mode}
        for j in range(len(self.mode)):
            if j not in forwarded:
                self.arrive(j)

    def drain(self):
        for j in range(len(self.mode)):
            self.copy(j, False).wait_send()


def run_gathers(pieces, lag=1.0):
    events = []
    for piece in pieces:
        for order, (depth, action) in enumerate(piece.events()):
            events.append((piece.number + lag * depth, order, piece.number, action))
    for _, _, _, action in sorted(events, key=lambda ev: ev[:3]):
        action()
    for piece in pieces:
        piece.finish()
    for piece in pieces:
        piece.drain()


def halves_of(ref, index_rows, rows, half, axis):
    return ref


def gather_kernel(plan, count, *refs):
    ins, outs = refs[:count], refs[count:2 * count]
    send, recv, local = refs[2 * count:]
    greet(ctx_neighbours())
    pieces, copies = [], []
    for number, (a, mode, first, rows) in enumerate(plan):
        out, width = outs[a], ins[a].shape[1]

        def slot(index, half, out=out, first=first, rows=rows, width=width):
            if half is None:
                return out.at[index, pl.ds(first, rows), :]
            part = rows // 2
            return out.at[index, pl.ds(first + half * part, part), :]

        own = ins[a].at[pl.ds(first, rows), :]
        pieces.append(Gather(number, mode, own, slot, send, recv))
        copies.append(pltpu.make_async_copy(own, slot(lax.axis_index("ctx"), None), local.at[number]))
    for copy in copies:
        copy.start()
    run_gathers(pieces)
    for copy in copies:
        copy.wait()


def gather_ctx(arrays, plan, collective_id, name):
    n = len(plan)
    return pl.pallas_call(
        functools.partial(gather_kernel, plan, len(arrays)),
        out_shape=[jax.ShapeDtypeStruct((16,) + a.shape, a.dtype) for a in arrays],
        in_specs=[pl.BlockSpec(memory_space=pl.ANY)] * len(arrays),
        out_specs=[pl.BlockSpec(memory_space=pl.ANY)] * len(arrays),
        scratch_shapes=[
            pltpu.SemaphoreType.DMA((n, N_TRANSFERS)),
            pltpu.SemaphoreType.DMA((n, N_TRANSFERS)),
            pltpu.SemaphoreType.DMA((n,)),
        ],
        compiler_params=pltpu.CompilerParams(collective_id=collective_id, has_side_effects=True),
        name=name,
    )(*arrays)


def rms_scale(matrix, gain_vec):
    widened = matrix.astype(jnp.float32)
    inverse = lax.rsqrt(jnp.mean(widened * widened, axis=-1, keepdims=True) + 1e-05)
    return (widened * inverse * gain_vec.astype(jnp.float32)).astype(jnp.bfloat16)


def rotate(matrix, positions, head_dim):
    row_count = matrix.shape[0]
    head_count = matrix.shape[1] // head_dim
    half_dim = head_dim // 2
    shaped = matrix.reshape(row_count, head_count, head_dim)
    frequency = jnp.exp(
        jnp.arange(half_dim).astype(jnp.float32) * (-2.0 * math.log(1000000.0) / head_dim)
    )
    angles = positions.astype(jnp.float32)[:, None] * frequency[None, :]
    cosine = jnp.cos(angles)[:, None, :]
    sine_part = jnp.sin(angles)[:, None, :]
    first_half = shaped[:, :, :half_dim]
    second_half = shaped[:, :, half_dim:]
    turned = jnp.concatenate(
        [
            first_half * cosine - second_half * sine_part,
            second_half * cosine + first_half * sine_part,
        ],
        axis=2,
    )
    return turned.reshape(row_count, head_count * head_dim)


def local(
    hidden_in,
    attn_gain,
    w_query,
    w_key,
    w_value,
    w_out,
    prior_keys,
    prior_values,
    stretch_offset,
    ffn_gain,
    w_gate,
    w_up,
    w_down,
    expert_ids,
    gate_weights,
):
    exp_count = lax.axis_size("exp")
    ctx_index = lax.axis_index("ctx")
    exp_index = lax.axis_index("exp")
    local_len = hidden_in.shape[0]
    model_width = hidden_in.shape[1]
    query_width = w_query.shape[1]
    key_width = w_key.shape[1]
    kv_local = key_width // HEAD_DIM
    head_group = HEADS // KV_HEADS
    normed = rms_scale(hidden_in, attn_gain)
    a, b = Y_THEN_X, X_THEN_Y
    gathered = gather_ctx(
        (w_key, w_value, w_query, prior_keys, prior_values, w_out),
        (
            (0, a, 0, 256), (1, b, 0, 256), (2, a, 0, 128), (2, b, 128, 128), (3, a, 0, 128), (4, b, 0, 128),
            (5, a, 0, 256), (5, b, 256, 256),
        ),
        0,
        "gather_weights",
    )
    portions = tuple(gathered[i].reshape(-1, gathered[i].shape[-1]) for i in (2, 0, 1))
    prior_k, prior_v = (gathered[i].reshape(-1, HEAD_DIM) for i in (3, 4))
    w_out_all = gathered[5].transpose(1, 0, 2).reshape(w_out.shape[0], -1)
    query_raw, key_raw, value_raw = tuple(
        (jnp.dot(normed, portion, preferred_element_type=jnp.float32) for portion in portions)
    )
    positions = stretch_offset[0] + ctx_index * local_len + jnp.arange(local_len, dtype=jnp.int32)
    query_rot = rotate(query_raw, positions, HEAD_DIM).astype(jnp.bfloat16)
    key_now = rotate(key_raw, positions, HEAD_DIM).astype(jnp.bfloat16)
    value_now = value_raw.astype(jnp.bfloat16)
    query_rows = (
        query_rot.reshape(local_len, kv_local, head_group, HEAD_DIM)
        .transpose(1, 0, 2, 3)
        .reshape(kv_local, local_len * head_group, HEAD_DIM)
    )
    query_pos = (
        ctx_index * local_len + jnp.arange(local_len * head_group, dtype=jnp.int32) // head_group
    )
    row_best = jnp.full((kv_local, local_len * head_group), -1e30, jnp.float32)
    now_k, now_v = gather_ctx((key_now, value_now), ((0, a, 0, 128), (1, b, 0, 128)), 1, "gather_kv")
    now_k, now_v = now_k.reshape(-1, key_width), now_v.reshape(-1, key_width)
    key_span = prior_k.shape[0]
    key_index = jnp.arange(key_span, dtype=jnp.int32)
    keys_cat = jnp.concatenate([prior_k, now_k], axis=0).reshape(2 * key_span, kv_local, HEAD_DIM)
    values_cat = jnp.concatenate([prior_v, now_v], axis=0).reshape(2 * key_span, kv_local, HEAD_DIM)
    scores = jnp.einsum(
        "hqd,khd->hqk", query_rows, keys_cat, preferred_element_type=jnp.float32
    ) / math.sqrt(HEAD_DIM)
    visible = jnp.concatenate(
        [key_index[None, :] > query_pos[:, None], key_index[None, :] <= query_pos[:, None]], axis=1
    )[None]
    scores = jnp.where(visible, scores, -1e30)
    new_best = jnp.maximum(row_best, jnp.max(scores, axis=2))
    weights = jnp.where(visible, jnp.exp(scores - new_best[:, :, None]), 0.0)
    row_mass = jnp.sum(weights, axis=2)
    weighted = jnp.einsum(
        "hqk,khd->hqd", weights.astype(jnp.bfloat16), values_cat, preferred_element_type=jnp.float32
    )
    row_best, row_mass, weighted = (new_best, row_mass, weighted)
    blended = weighted / row_mass[:, :, None]
    attended = (
        blended.reshape(kv_local, local_len, head_group, HEAD_DIM)
        .transpose(1, 0, 2, 3)
        .reshape(local_len, query_width)
        .astype(jnp.bfloat16)
    )
    head_part = jnp.dot(
        attended,
        w_out_all,
        preferred_element_type=jnp.float32,
    )
    summed = lax.psum_scatter(
        head_part.astype(jnp.bfloat16), "exp", scatter_dimension=0, tiled=True
    ).astype(jnp.float32)
    tok_dev = local_len // exp_count
    own_rows = lax.dynamic_slice_in_dim(hidden_in, exp_index * tok_dev, tok_dev, 0)
    residual = (own_rows.astype(jnp.float32) + summed).astype(jnp.bfloat16)
    normed_ffn = rms_scale(residual, ffn_gain)
    capacity = 4 * tok_dev // exp_count
    device_row = (ctx_index * exp_count + exp_index) * tok_dev
    my_ids = lax.dynamic_slice_in_dim(expert_ids, device_row, tok_dev, 0).reshape(-1)
    onehot = (my_ids[:, None] == jnp.arange(exp_count, dtype=jnp.int32)[None, :]).astype(jnp.int32)
    before = jnp.cumsum(onehot, axis=0) - onehot
    slot_of = jnp.sum(before * onehot, axis=1)
    slot_ids = jnp.arange(exp_count * capacity, dtype=jnp.int32)
    select = (
        (slot_ids[:, None] // capacity == my_ids[None, :])
        & (slot_ids[:, None] % capacity == slot_of[None, :])
    ).astype(jnp.bfloat16)
    repeated = jnp.repeat(normed_ffn, 2, axis=0)
    outgoing = (
        jnp.dot(select, repeated, preferred_element_type=jnp.float32)
        .astype(jnp.bfloat16)
        .reshape(exp_count, capacity, model_width)
    )
    arrived = lax.all_to_all(outgoing, "exp", split_axis=0, concat_axis=0, tiled=True)
    gate_mat = w_gate[0]
    up_mat = w_up[0]
    down_mat = w_down[0]
    flattened = gather_ctx(
        (arrived.reshape(-1, model_width),),
        ((0, a, 0, 32), (0, b, 32, 32)),
        2,
        "gather_tokens",
    )[0].reshape(-1, model_width)
    gate_part = jnp.dot(flattened, gate_mat, preferred_element_type=jnp.float32)
    up_part = jnp.dot(flattened, up_mat, preferred_element_type=jnp.float32)
    hidden_act = (jax.nn.silu(gate_part) * up_part).astype(jnp.bfloat16)
    own_slots = lax.psum_scatter(
        jnp.dot(hidden_act, down_mat, preferred_element_type=jnp.float32).astype(jnp.bfloat16),
        "ctx",
        scatter_dimension=0,
        tiled=True,
    )
    outcome = own_slots.reshape(exp_count, capacity, model_width)
    returned = lax.all_to_all(outcome, "exp", split_axis=0, concat_axis=0, tiled=True)
    gathered_back = jnp.dot(
        select.T,
        returned.reshape(exp_count * capacity, model_width),
        preferred_element_type=jnp.float32,
    )
    picked = gathered_back.reshape(tok_dev, 2, model_width)
    mixture = jnp.sum(gate_weights[:, :, None] * picked, axis=1)
    return (residual.astype(jnp.float32) + mixture).astype(jnp.bfloat16)


def solution(mesh):
    in_specs = (
        P("ctx", None),
        P(),
        P("ctx", "exp"),
        P("ctx", "exp"),
        P("ctx", "exp"),
        P("exp", "ctx"),
        P("ctx", "exp"),
        P("ctx", "exp"),
        P(),
        P(),
        P("exp", None, "ctx"),
        P("exp", None, "ctx"),
        P("exp", "ctx", None),
        P(),
        P(("ctx", "exp"), None),
    )
    out_specs = P(("ctx", "exp"), None)
    return jax.shard_map(local, mesh=mesh, in_specs=in_specs, out_specs=out_specs, check_vma=False)
```

```python
import functools
import math

import jax
import jax.numpy as jnp
from jax import lax
from jax.experimental import pallas as pl
from jax.experimental.pallas import tpu as pltpu
from jax.sharding import PartitionSpec as P

HEADS = 32
KV_HEADS = 8
HEAD_DIM = 128
MESH = pl.DeviceIdType.MESH
NX, NY, NK = 4, 2, 2

Y_THEN_X = (
    (None, (0, 0, 0), None, "Y"),
    (None, (0, 0, 0), None, "R"),
    (None, (0, 0, 0), None, "L"),
    (None, (0, 0, 0), None, "S"),
    (0, (0, 1, 0), None, "R"),
    (0, (0, 1, 0), None, "L"),
    (0, (0, 1, 0), None, "S"),
    (1, (-1, 0, 0), 0, "R"),
    (1, (-1, 0, 0), None, "S"),
    (2, (1, 0, 0), 1, "L"),
    (2, (1, 0, 0), None, "S"),
    (4, (-1, 1, 0), 0, "R"),
    (4, (-1, 1, 0), None, "S"),
    (5, (1, 1, 0), 1, "L"),
    (5, (1, 1, 0), None, "S"),
    (7, (2, 0, 0), 0, "S"),
    (9, (2, 0, 0), 1, "S"),
    (11, (2, 1, 0), 0, "S"),
    (13, (2, 1, 0), 1, "S"),
)
X_THEN_Y = (
    (None, (0, 0, 0), None, "R"),
    (None, (0, 0, 0), None, "L"),
    (None, (0, 0, 0), None, "Y"),
    (None, (0, 0, 0), None, "S"),
    (0, (-1, 0, 0), 0, "R"),
    (0, (-1, 0, 0), None, "Y"),
    (0, (-1, 0, 0), None, "S"),
    (1, (1, 0, 0), 1, "L"),
    (1, (1, 0, 0), None, "Y"),
    (1, (1, 0, 0), None, "S"),
    (2, (0, 1, 0), None, "S"),
    (4, (2, 0, 0), 0, "Y"),
    (4, (2, 0, 0), 0, "S"),
    (7, (2, 0, 0), 1, "Y"),
    (7, (2, 0, 0), 1, "S"),
    (5, (-1, 1, 0), None, "S"),
    (8, (1, 1, 0), None, "S"),
    (11, (2, 1, 0), 0, "S"),
    (13, (2, 1, 0), 1, "S"),
)
DIRECT = tuple((None, (0, 0, 0), None, to) for to in ("R", "L", "Y", "O", "RY", "LY", "OY", "S")) + (
    (0, (-1, 0, 0), None, "S"),
    (1, (1, 0, 0), None, "S"),
    (2, (0, 1, 0), None, "S"),
    (3, (2, 0, 0), None, "S"),
    (4, (-1, 1, 0), None, "S"),
    (5, (1, 1, 0), None, "S"),
    (6, (2, 1, 0), None, "S"),
)
N_TRANSFERS = 19
STEP = {
    "R": (1, 0, 0), "L": (-1, 0, 0), "Y": (0, 1, 0), "S": (0, 0, 1),
    "O": (2, 0, 0), "RY": (1, 1, 0), "LY": (-1, 1, 0), "OY": (2, 1, 0),
}
FROM = {to: (-step[0], step[1], step[2]) for to, step in STEP.items()}


def ctx_at(delta):
    c = lax.axis_index("ctx")
    x = (c // 4 + delta[0] + NX) % NX
    y = ((c // 2) % 2 + delta[1]) % NY
    k = (c % 2 + delta[2]) % NK
    return x * 4 + y * 2 + k


def plus(a, b):
    return ((a[0] + b[0]) % NX, (a[1] + b[1]) % NY, (a[2] + b[2]) % NK)


def greet(targets):
    barrier = pltpu.get_barrier_semaphore()
    for target in targets:
        pl.semaphore_signal(barrier, inc=1, device_id=target, device_id_type=MESH)
    pl.semaphore_wait(barrier, len(targets))


def ctx_neighbours():
    e = lax.axis_index("exp")
    return [(ctx_at(STEP[t]), e) for t in "RLYS"]


class Gather:
    def __init__(self, number, mode, slot, send, recv):
        self.number, self.mode, self.slot = number, mode, slot
        self.send, self.recv = send, recv
        self.depth = []
        for trigger, _, _, _ in mode:
            self.depth.append(0 if trigger is None else self.depth[trigger] + 1)

    def copy(self, j, arriving):
        trigger, rel, half, to = self.mode[j]
        e = lax.axis_index("exp")
        at = plus(FROM[to], rel) if arriving else rel
        ref = self.slot(ctx_at(at), half)
        source = ref
        return pltpu.make_async_remote_copy(
            src_ref=source,
            dst_ref=ref,
            send_sem=self.send.at[self.number, j],
            recv_sem=self.recv.at[self.number, j],
            device_id=(ctx_at(STEP[to]), e),
            device_id_type=MESH,
        )

    def start(self, trigger):
        for j, transfer in enumerate(self.mode):
            if transfer[0] == trigger:
                self.copy(j, False).start()

    def arrive(self, j):
        self.copy(j, True).wait_recv()

    def events(self):
        triggers = sorted({t[0] for t in self.mode if t[0] is not None})
        out = [(0, functools.partial(self.start, None))]

        def forward(j):
            self.arrive(j)
            self.start(j)

        for j in triggers:
            out.append((self.depth[j] + 1, functools.partial(forward, j)))
        return out

    def finish(self):
        forwarded = {t[0] for t in self.mode}
        for j in range(len(self.mode)):
            if j not in forwarded:
                self.arrive(j)

    def drain(self):
        for j in range(len(self.mode)):
            self.copy(j, False).wait_send()


CHUNKS = (((0, 0), (0, 1)), ((3, 0), (1, 0)), ((3, 1), (1, 1)), ((2, 0), (2, 1)))
PLACE = {}
for _g, _pair in enumerate(CHUNKS):
    for _i, _xy in enumerate(_pair):
        for _dk in range(2):
            PLACE[_xy + (_dk,)] = (_g, _dk * 2 + _i)
ROWS = 64
GU = 128
DN = 512


class LocalGather(Gather):
    def copy(self, j, arriving):
        trigger, rel, half, to = self.mode[j]
        e = lax.axis_index("exp")
        there = plus(FROM[to], rel)
        here = there if arriving else plus(rel, (0, 0, 0))
        return pltpu.make_async_remote_copy(
            src_ref=self.slot(here, half),
            dst_ref=self.slot(there, half),
            send_sem=self.send.at[self.number, j],
            recv_sem=self.recv.at[self.number, j],
            device_id=(ctx_at(STEP[to]), e),
            device_id_type=MESH,
        )


def expert_kernel(
    arrived, gate, up, down, out,
    tok, wgu, wdn, hid, part, from_sib, from_x, from_y,
    ag_send, ag_recv, w_sem, own_sem, rs_send, rs_recv,
):
    e = lax.axis_index("exp")
    units = gate.shape[2] // GU
    width = down.shape[2]
    own_copy = pltpu.make_async_copy(arrived, tok.at[0, pl.ds(0, ROWS), :], own_sem)
    own_copy.start()
    loads = []
    for j in range(units):
        for s, w in enumerate((gate, up)):
            loads.append(
                pltpu.make_async_copy(
                    w.at[0, :, pl.ds(j * GU, GU)], wgu.at[j, :, pl.ds(s * GU, GU)], w_sem.at[2 * j + s]
                )
            )
    loads.append(pltpu.make_async_copy(down.at[0], wdn, w_sem.at[2 * units]))
    greet(ctx_neighbours() + [(ctx_at((2, 0, 0)), e)])
    own_copy.wait()

    pieces = []
    for number, mode in enumerate((Y_THEN_X, X_THEN_Y)):
        rows = ROWS // 2

        def slot(rel, half, first=number * rows, rows=rows):
            g, place = PLACE[rel]
            if half is None:
                return tok.at[g, pl.ds(place * ROWS + first, rows), :]
            return tok.at[g, pl.ds(place * ROWS + first + half * (rows // 2), rows // 2), :]

        pieces.append(LocalGather(number, mode, slot, ag_send, ag_recv))
    first, second = pieces
    for piece in pieces:
        piece.start(None)
    for load in loads:
        load.start()

    def forward(piece, *js):
        for j in js:
            piece.arrive(j)
            piece.start(j)

    def need(piece, *js):
        for j in js:
            piece.arrive(j)

    def gate_up(g, lo, hi):
        def body(j, _):
            both = jnp.dot(tok[g], wgu[j], preferred_element_type=jnp.float32)
            v = both[:, :GU]
            hid[:, pl.ds(pl.multiple_of(j * GU, GU), GU)] = (v / (1.0 + jnp.exp(-v)) * both[:, GU:]).astype(jnp.bfloat16)
            return 0

        lax.fori_loop(lo, hi, body, 0)

    def down_part(g, lo, hi):
        def body(n, _):
            cols = pl.ds(pl.multiple_of(n * DN, DN), DN)
            part[g, :, cols] = jnp.dot(hid[...], wdn[:, cols], preferred_element_type=jnp.float32).astype(jnp.bfloat16)
            return 0

        lax.fori_loop(lo, hi, body, 0)

    def rs_copy(j, source, target, to):
        return pltpu.make_async_remote_copy(
            src_ref=source, dst_ref=target, send_sem=rs_send.at[j], recv_sem=rs_recv.at[j],
            device_id=(ctx_at(to), e), device_id_type=MESH,
        )

    half = 2 * ROWS
    to_sib = [
        rs_copy(g, part.at[g, pl.ds(half, half), :], from_sib.at[g], (0, 0, 1)) for g in range(4)
    ]
    near, far = pl.ds(0, ROWS), pl.ds(ROWS, ROWS)
    to_x = {
        1: [
            rs_copy(4, part.at[1, near, :], from_x.at[0, 0], (-1, 0, 0)),
            rs_copy(5, part.at[1, far, :], from_x.at[1, 0], (1, 0, 0)),
        ],
        2: [
            rs_copy(6, part.at[2, near, :], from_x.at[0, 1], (-1, 0, 0)),
            rs_copy(7, part.at[2, far, :], from_x.at[1, 1], (1, 0, 0)),
        ],
        3: [
            rs_copy(8, part.at[3, far, :], from_x.at[2, 1], (2, 0, 0)),
            rs_copy(9, part.at[3, near, :], from_x.at[2, 0], (2, 0, 0)),
        ],
    }
    to_y = rs_copy(10, part.at[0, far, :], from_y, (0, 1, 0))
    tile = 16

    def add_rows(rows, terms, store):
        def body(i, _):
            at = pl.multiple_of(i * tile, tile)
            total = terms[0](at)
            for term in terms[1:]:
                total = total + term(at)
            store(at, total.astype(jnp.bfloat16))
            return 0

        lax.fori_loop(0, rows // tile, body, 0)

    def merge(g):
        to_sib[g].wait_recv()

        def store(at, value):
            part[g, pl.ds(at, tile), :] = value

        add_rows(
            half,
            [
                lambda at: part[g, pl.ds(at, tile), :].astype(jnp.float32),
                lambda at: from_sib[g, pl.ds(at, tile), :].astype(jnp.float32),
            ],
            store,
        )
        for copy in to_x.get(g, ()):
            copy.start()

    forward(first, 0)
    forward(second, 2)
    need(first, 3, 6)
    need(second, 3, 10)
    for load in loads[:-1]:
        load.wait()
    gate_up(0, 0, 4)
    forward(first, 1, 2)
    forward(second, 0, 1)
    gate_up(0, 4, units)
    loads[-1].wait()
    forward(first, 4, 5)
    down_part(0, 0, width // DN)
    to_sib[0].start()
    forward(second, 4, 7)
    forward(second, 5, 8)
    need(first, 8, 10)
    need(second, 6, 9)
    gate_up(1, 0, 4)
    forward(first, 7, 9)
    gate_up(1, 4, units)
    forward(second, 11, 13)
    down_part(1, 0, width // DN)
    to_sib[1].start()
    merge(0)
    forward(first, 11, 13)
    need(first, 12, 14)
    need(second, 15, 16)
    gate_up(2, 0, units)
    merge(1)
    down_part(2, 0, width // DN)
    to_sib[2].start()
    need(first, 15, 16, 17, 18)
    need(second, 12, 14, 17, 18)
    gate_up(3, 0, units)
    merge(2)
    down_part(3, 0, width // DN)
    to_sib[3].start()
    merge(3)

    to_x[2][0].wait_recv()
    to_x[2][1].wait_recv()
    to_x[3][0].wait_recv()

    def store_far(at, value):
        part[0, pl.ds(ROWS + at, tile), :] = value

    add_rows(
        ROWS,
        [lambda at: part[0, pl.ds(ROWS + at, tile), :].astype(jnp.float32)]
        + [lambda at, s=s: from_x[s, 1, pl.ds(at, tile), :].astype(jnp.float32) for s in range(3)],
        store_far,
    )
    to_y.start()
    to_x[1][0].wait_recv()
    to_x[1][1].wait_recv()
    to_x[3][1].wait_recv()
    to_y.wait_recv()

    def store_out(at, value):
        out[pl.ds(at, tile), :] = value

    add_rows(
        ROWS,
        [lambda at: part[0, pl.ds(at, tile), :].astype(jnp.float32)]
        + [lambda at, s=s: from_x[s, 0, pl.ds(at, tile), :].astype(jnp.float32) for s in range(3)]
        + [lambda at: from_y[pl.ds(at, tile), :].astype(jnp.float32)],
        store_out,
    )
    for piece in pieces:
        piece.drain()
    for copy in to_sib + to_x[1] + to_x[2] + to_x[3] + [to_y]:
        copy.wait_send()


def experts(arrived, w_gate, w_up, w_down):
    rows, width = arrived.shape
    ff = w_gate.shape[2]
    bf16 = jnp.bfloat16
    return pl.pallas_call(
        expert_kernel,
        out_shape=jax.ShapeDtypeStruct((rows, width), bf16),
        in_specs=[pl.BlockSpec(memory_space=pl.ANY)] * 4,
        out_specs=pl.BlockSpec(memory_space=pltpu.VMEM),
        scratch_shapes=[
            pltpu.VMEM((4, 4 * rows, width), bf16),
            pltpu.VMEM((ff // GU, width, 2 * GU), bf16),
            pltpu.VMEM((ff, width), bf16),
            pltpu.VMEM((4 * rows, ff), bf16),
            pltpu.VMEM((4, 4 * rows, width), bf16),
            pltpu.VMEM((4, 2 * rows, width), bf16),
            pltpu.VMEM((3, 2, rows, width), bf16),
            pltpu.VMEM((rows, width), bf16),
            pltpu.SemaphoreType.DMA((2, N_TRANSFERS)),
            pltpu.SemaphoreType.DMA((2, N_TRANSFERS)),
            pltpu.SemaphoreType.DMA((2 * (ff // GU) + 1,)),
            pltpu.SemaphoreType.DMA,
            pltpu.SemaphoreType.DMA((11,)),
            pltpu.SemaphoreType.DMA((11,)),
        ],
        compiler_params=pltpu.CompilerParams(
            collective_id=3, has_side_effects=True, vmem_limit_bytes=56 * 1024 * 1024
        ),
        name="experts",
    )(arrived, w_gate, w_up, w_down)

def mixer_kernel(
    hidden, attn_gain, w_query, w_key, w_value, w_out, prior_keys, prior_values, cosine, sine, ffn_gain,
    residual_out, normed_out,
    normed, wkv, wq, kv, wo, query, scores, best, mass, blend, attended, part, from_exp,
    send, recv, local, rs_send, rs_recv,
):
    c, e = lax.axis_index("ctx"), lax.axis_index("exp")
    f32, bf16 = jnp.float32, jnp.bfloat16
    tokens, width = hidden.shape
    depth = w_query.shape[0]
    heads = w_query.shape[1] // HEAD_DIM
    tok_dev = residual_out.shape[0]
    out_cols = w_out.shape[1]
    span = kv.shape[0] // 2

    own_rows = pl.ds(pl.multiple_of(c * depth, depth), depth)
    own_keys = pl.ds(pl.multiple_of(c * tokens, tokens), tokens)
    left, right = pl.ds(0, HEAD_DIM), pl.ds(HEAD_DIM, HEAD_DIM)
    copies = [
        pltpu.make_async_copy(source, target, local.at[i])
        for i, (source, target) in enumerate(
            (
                (w_key, wkv.at[own_rows, left]),
                (w_value, wkv.at[own_rows, right]),
                (prior_keys, kv.at[own_keys, left]),
                (prior_values, kv.at[own_keys, right]),
                (w_query, wq.at[own_rows, :]),
                (w_out, wo.at[c]),
            )
        )
    ]
    for copy in copies:
        copy.start()
    greet(
        [(ctx_at(step), e) for step in STEP.values()] + [(c, lax.rem(e + d, 8)) for d in range(1, 8)]
    )
    for copy in copies:
        copy.wait()

    def rows_of(buffer, stride, base, first, rows):
        def slot(index, half):
            part_rows = rows if half is None else rows // 2
            start = base + index * stride + first + (0 if half is None else half * part_rows)
            return buffer.at[pl.ds(pl.multiple_of(start, 16), part_rows), :]

        return slot

    def block_of(buffer, first, rows):
        def slot(index, half):
            part_rows = rows if half is None else rows // 2
            return buffer.at[index, pl.ds(first + (0 if half is None else half * part_rows), part_rows), :]

        return slot

    plan = []
    for buffer, stride in ((wkv, depth), (kv, tokens), (wq, depth)):
        for i, mode in enumerate((Y_THEN_X, X_THEN_Y)):
            plan.append((mode, rows_of(buffer, stride, 0, i * stride // 2, stride // 2)))
    for i, mode in enumerate((Y_THEN_X, X_THEN_Y)):
        rows = w_out.shape[0] // 2
        plan.append((mode, block_of(wo, i * rows, rows)))
    pieces = [Gather(n, mode, slot, send, recv) for n, (mode, slot) in enumerate(plan)]
    now = Gather(len(pieces), DIRECT, rows_of(kv, tokens, span, 0, tokens), send, recv)

    tile = 16

    def norm_rows(i, _):
        rows = pl.ds(pl.multiple_of(i * tile, tile), tile)
        wide = hidden[rows, :].astype(f32)
        inverse = lax.rsqrt(jnp.mean(wide * wide, axis=-1, keepdims=True) + 1e-05)
        normed[rows, :] = (wide * inverse * attn_gain[...].astype(f32)).astype(bf16)
        return 0

    def normalise():
        lax.fori_loop(0, tokens // tile, norm_rows, 0)

    def turned(a):
        return (a * cosine[...] + pltpu.roll(a, HEAD_DIM // 2, 1) * sine[...]).astype(bf16)

    def keys_and_values():
        for piece in pieces[:2]:
            piece.finish()
        both = jnp.dot(normed[...], wkv[...], preferred_element_type=f32)
        rows = pl.ds(pl.multiple_of(span + c * tokens, tokens), tokens)
        kv[rows, left] = turned(both[:, :HEAD_DIM])
        kv[rows, right] = both[:, HEAD_DIM:].astype(bf16)
        now.start(None)

    def queries():
        for piece in pieces[4:6]:
            piece.finish()
        for g in range(heads):
            raw = jnp.dot(normed[...], wq[:, pl.ds(g * HEAD_DIM, HEAD_DIM)], preferred_element_type=f32)
            query[pl.ds(g * tokens, tokens), :] = turned(raw)

    count = heads * tokens
    block = 2 * tokens
    blocks = span // block
    inverse_root = 1.0 / math.sqrt(HEAD_DIM)

    def score(start, size):
        keys = kv[pl.ds(pl.multiple_of(start, tokens), size), left]
        return lax.dot_general(query[...], keys, (((1,), (1,)), ((), ())), preferred_element_type=f32) * inverse_root

    def masks():
        row = lax.broadcasted_iota(jnp.int32, (count, tokens), 0) % tokens
        col = lax.broadcasted_iota(jnp.int32, (count, tokens), 1)
        return row, col

    def all_scores():
        for piece in pieces[2:4] + [now]:
            piece.finish()
        row, col = masks()
        first = score(c * tokens, block)
        head_part = jnp.where(col > row, first[:, :tokens], -1e30)
        scores[:, pl.ds(0, tokens)] = head_part
        scores[:, pl.ds(tokens, tokens)] = first[:, tokens:]
        last = jnp.where(col <= row, score(c * tokens + span, tokens), -1e30)
        scores[:, pl.ds(span, tokens)] = last
        best[...] = jnp.maximum(jnp.maximum(head_part, first[:, tokens:]), last)

        def body(b, _):
            s = score(c * tokens + b * block, block)
            scores[:, pl.ds(pl.multiple_of(b * block, block), block)] = s
            best[...] = jnp.maximum(best[...], jnp.maximum(s[:, :tokens], s[:, tokens:]))
            return 0

        lax.fori_loop(1, blocks, body, 0)
        best[...] = jnp.broadcast_to(jnp.max(best[...], axis=1, keepdims=True), best.shape)

    def blended():
        top = best[:, pl.ds(0, 1)]
        p = jnp.exp(scores[:, pl.ds(span, tokens)] - top)
        mass[...] = p
        values = kv[pl.ds(pl.multiple_of(c * tokens + span, tokens), tokens), right]
        blend[...] = jnp.dot(p.astype(bf16), values, preferred_element_type=f32)

        def body(b, _):
            p = jnp.exp(scores[:, pl.ds(pl.multiple_of(b * block, block), block)] - top)
            mass[...] += p[:, :tokens] + p[:, tokens:]
            values = kv[pl.ds(pl.multiple_of(c * tokens + b * block, tokens), block), right]
            blend[...] += jnp.dot(p.astype(bf16), values, preferred_element_type=f32)
            return 0

        lax.fori_loop(0, blocks, body, 0)
        result = (blend[...] / jnp.sum(mass[...], axis=1, keepdims=True)).astype(bf16)
        for g in range(heads):
            attended[:, pl.ds(g * HEAD_DIM, HEAD_DIM)] = result[g * tokens:(g + 1) * tokens, :]

    def forward_now():
        for j in range(7):
            now.arrive(j)
            now.start(j)

    timeline = []
    for piece in pieces:
        for order, (level, action) in enumerate(piece.events()):
            timeline.append((piece.number + 1.0 * level, order, action))
    timeline += [
        (1.5, 0, normalise),
        (4.5, 0, keys_and_values),
        (7.5, 0, forward_now),
        (8.5, 0, queries),
        (8.6, 0, all_scores),
        (9.5, 0, blended),
    ]
    for _, _, action in sorted(timeline, key=lambda item: item[:2]):
        action()
    for piece in pieces[6:]:
        piece.finish()

    def project(i, _):
        cols = pl.ds(pl.multiple_of(i * out_cols, out_cols), out_cols)
        part[:, cols] = jnp.dot(attended[...], wo[i], preferred_element_type=f32).astype(bf16)
        return 0

    lax.fori_loop(0, width // out_cols, project, 0)

    shares = []
    for d in range(1, 8):
        to = lax.rem(e + d, 8)
        shares.append(
            pltpu.make_async_remote_copy(
                src_ref=part.at[pl.ds(pl.multiple_of(to * tok_dev, tok_dev), tok_dev), :],
                dst_ref=from_exp.at[d - 1],
                send_sem=rs_send.at[d - 1],
                recv_sem=rs_recv.at[d - 1],
                device_id=(c, to),
                device_id_type=MESH,
            )
        )
    for share in shares:
        share.start()
    for share in shares:
        share.wait_recv()
    mine = pl.ds(pl.multiple_of(e * tok_dev, tok_dev), tok_dev)
    total = part[mine, :].astype(f32)
    for d in range(7):
        total = total + from_exp[d].astype(f32)
    residual = (hidden[mine, :].astype(f32) + total).astype(bf16)
    residual_out[...] = residual
    wide = residual.astype(f32)
    inverse = lax.rsqrt(jnp.mean(wide * wide, axis=-1, keepdims=True) + 1e-05)
    normed_out[...] = (wide * inverse * ffn_gain[...].astype(f32)).astype(bf16)
    for piece in pieces + [now]:
        piece.drain()
    for share in shares:
        share.wait_send()


def mixer(hidden, attn_gain, w_query, w_key, w_value, w_out, prior_keys, prior_values, cosine, sine, ffn_gain):
    tokens, width = hidden.shape
    depth, q_cols = w_query.shape
    bf16, f32 = jnp.bfloat16, jnp.float32
    span = 16 * tokens
    count = q_cols // HEAD_DIM * tokens
    vmem = pl.BlockSpec(memory_space=pltpu.VMEM)
    anywhere = pl.BlockSpec(memory_space=pl.ANY)
    return pl.pallas_call(
        mixer_kernel,
        out_shape=[jax.ShapeDtypeStruct((tokens // 8, width), bf16)] * 2,
        in_specs=[vmem, vmem] + [anywhere] * 6 + [vmem] * 3,
        out_specs=[vmem] * 2,
        scratch_shapes=[
            pltpu.VMEM((tokens, width), bf16),
            pltpu.VMEM((16 * depth, 2 * HEAD_DIM), bf16),
            pltpu.VMEM((16 * depth, q_cols), bf16),
            pltpu.VMEM((2 * span, 2 * HEAD_DIM), bf16),
            pltpu.VMEM((16,) + w_out.shape, bf16),
            pltpu.VMEM((count, HEAD_DIM), bf16),
            pltpu.VMEM((count, span + tokens), f32),
            pltpu.VMEM((count, tokens), f32),
            pltpu.VMEM((count, tokens), f32),
            pltpu.VMEM((count, HEAD_DIM), f32),
            pltpu.VMEM((tokens, q_cols), bf16),
            pltpu.VMEM((tokens, width), bf16),
            pltpu.VMEM((7, tokens // 8, width), bf16),
            pltpu.SemaphoreType.DMA((9, N_TRANSFERS)),
            pltpu.SemaphoreType.DMA((9, N_TRANSFERS)),
            pltpu.SemaphoreType.DMA((6,)),
            pltpu.SemaphoreType.DMA((7,)),
            pltpu.SemaphoreType.DMA((7,)),
        ],
        compiler_params=pltpu.CompilerParams(
            collective_id=0, has_side_effects=True, vmem_limit_bytes=48 * 1024 * 1024
        ),
        name="mixer",
    )(hidden, attn_gain, w_query, w_key, w_value, w_out, prior_keys, prior_values, cosine, sine, ffn_gain)


def local(
    hidden_in,
    attn_gain,
    w_query,
    w_key,
    w_value,
    w_out,
    prior_keys,
    prior_values,
    stretch_offset,
    ffn_gain,
    w_gate,
    w_up,
    w_down,
    expert_ids,
    gate_weights,
):
    exp_count = lax.axis_size("exp")
    ctx_index = lax.axis_index("ctx")
    exp_index = lax.axis_index("exp")
    local_len, model_width = hidden_in.shape
    tok_dev = local_len // exp_count
    positions = stretch_offset[0] + ctx_index * local_len + jnp.arange(local_len, dtype=jnp.int32)
    half_dim = HEAD_DIM // 2
    frequency = jnp.exp(jnp.arange(half_dim).astype(jnp.float32) * (-2.0 * math.log(1000000.0) / HEAD_DIM))
    angles = positions.astype(jnp.float32)[:, None] * frequency[None, :]
    cosine, sine = jnp.cos(angles), jnp.sin(angles)
    residual, normed_ffn = mixer(
        hidden_in,
        attn_gain[None],
        w_query,
        w_key,
        w_value,
        w_out,
        prior_keys,
        prior_values,
        jnp.concatenate([cosine, cosine], axis=1),
        jnp.concatenate([-sine, sine], axis=1),
        ffn_gain[None],
    )
    capacity = 4 * tok_dev // exp_count
    device_row = (ctx_index * exp_count + exp_index) * tok_dev
    my_ids = lax.dynamic_slice_in_dim(expert_ids, device_row, tok_dev, 0).reshape(-1)
    onehot = (my_ids[:, None] == jnp.arange(exp_count, dtype=jnp.int32)[None, :]).astype(jnp.int32)
    before = jnp.cumsum(onehot, axis=0) - onehot
    slot_of = jnp.sum(before * onehot, axis=1)
    slot_ids = jnp.arange(exp_count * capacity, dtype=jnp.int32)
    select = (
        (slot_ids[:, None] // capacity == my_ids[None, :])
        & (slot_ids[:, None] % capacity == slot_of[None, :])
    ).astype(jnp.bfloat16)
    repeated = jnp.repeat(normed_ffn, 2, axis=0)
    outgoing = (
        jnp.dot(select, repeated, preferred_element_type=jnp.float32)
        .astype(jnp.bfloat16)
        .reshape(exp_count, capacity, model_width)
    )
    arrived = lax.all_to_all(outgoing, "exp", split_axis=0, concat_axis=0, tiled=True)
    own_slots = experts(arrived.reshape(-1, model_width), w_gate, w_up, w_down)
    outcome = own_slots.reshape(exp_count, capacity, model_width)
    returned = lax.all_to_all(outcome, "exp", split_axis=0, concat_axis=0, tiled=True)
    gathered_back = jnp.dot(
        select.T,
        returned.reshape(exp_count * capacity, model_width),
        preferred_element_type=jnp.float32,
    )
    picked = gathered_back.reshape(tok_dev, 2, model_width)
    mixture = jnp.sum(gate_weights[:, :, None] * picked, axis=1)
    return (residual.astype(jnp.float32) + mixture).astype(jnp.bfloat16)


def solution(mesh):
    in_specs = (
        P("ctx", None),
        P(),
        P("ctx", "exp"),
        P("ctx", "exp"),
        P("ctx", "exp"),
        P("exp", "ctx"),
        P("ctx", "exp"),
        P("ctx", "exp"),
        P(),
        P(),
        P("exp", None, "ctx"),
        P("exp", None, "ctx"),
        P("exp", "ctx", None),
        P(),
        P(("ctx", "exp"), None),
    )
    out_specs = P(("ctx", "exp"), None)
    return jax.shard_map(local, mesh=mesh, in_specs=in_specs, out_specs=out_specs, check_vma=False)
```

```python
import functools
import math

import jax
import jax.numpy as jnp
from jax import lax
from jax.experimental import pallas as pl
from jax.experimental.pallas import tpu as pltpu
from jax.sharding import PartitionSpec as P

HEADS = 32
KV_HEADS = 8
HEAD_DIM = 128
MESH = pl.DeviceIdType.MESH
NX, NY, NK = 4, 2, 2

Y_THEN_X = (
    (None, (0, 0, 0), None, "Y"),
    (None, (0, 0, 0), None, "R"),
    (None, (0, 0, 0), None, "L"),
    (None, (0, 0, 0), None, "S"),
    (0, (0, 1, 0), None, "R"),
    (0, (0, 1, 0), None, "L"),
    (0, (0, 1, 0), None, "S"),
    (1, (-1, 0, 0), 0, "R"),
    (1, (-1, 0, 0), None, "S"),
    (2, (1, 0, 0), 1, "L"),
    (2, (1, 0, 0), None, "S"),
    (4, (-1, 1, 0), 0, "R"),
    (4, (-1, 1, 0), None, "S"),
    (5, (1, 1, 0), 1, "L"),
    (5, (1, 1, 0), None, "S"),
    (7, (2, 0, 0), 0, "S"),
    (9, (2, 0, 0), 1, "S"),
    (11, (2, 1, 0), 0, "S"),
    (13, (2, 1, 0), 1, "S"),
)
X_THEN_Y = (
    (None, (0, 0, 0), None, "R"),
    (None, (0, 0, 0), None, "L"),
    (None, (0, 0, 0), None, "Y"),
    (None, (0, 0, 0), None, "S"),
    (0, (-1, 0, 0), 0, "R"),
    (0, (-1, 0, 0), None, "Y"),
    (0, (-1, 0, 0), None, "S"),
    (1, (1, 0, 0), 1, "L"),
    (1, (1, 0, 0), None, "Y"),
    (1, (1, 0, 0), None, "S"),
    (2, (0, 1, 0), None, "S"),
    (4, (2, 0, 0), 0, "Y"),
    (4, (2, 0, 0), 0, "S"),
    (7, (2, 0, 0), 1, "Y"),
    (7, (2, 0, 0), 1, "S"),
    (5, (-1, 1, 0), None, "S"),
    (8, (1, 1, 0), None, "S"),
    (11, (2, 1, 0), 0, "S"),
    (13, (2, 1, 0), 1, "S"),
)
DIRECT = tuple((None, (0, 0, 0), None, to) for to in ("R", "L", "Y", "O", "RY", "LY", "OY", "S")) + (
    (0, (-1, 0, 0), None, "S"),
    (1, (1, 0, 0), None, "S"),
    (2, (0, 1, 0), None, "S"),
    (3, (2, 0, 0), None, "S"),
    (4, (-1, 1, 0), None, "S"),
    (5, (1, 1, 0), None, "S"),
    (6, (2, 1, 0), None, "S"),
)
N_TRANSFERS = 19
STEP = {
    "R": (1, 0, 0), "L": (-1, 0, 0), "Y": (0, 1, 0), "S": (0, 0, 1),
    "O": (2, 0, 0), "RY": (1, 1, 0), "LY": (-1, 1, 0), "OY": (2, 1, 0),
}
FROM = {to: (-step[0], step[1], step[2]) for to, step in STEP.items()}


def ctx_at(delta):
    c = lax.axis_index("ctx")
    x = (c // 4 + delta[0] + NX) % NX
    y = ((c // 2) % 2 + delta[1]) % NY
    k = (c % 2 + delta[2]) % NK
    return x * 4 + y * 2 + k


def plus(a, b):
    return ((a[0] + b[0]) % NX, (a[1] + b[1]) % NY, (a[2] + b[2]) % NK)


def greet(targets):
    barrier = pltpu.get_barrier_semaphore()
    for target in targets:
        pl.semaphore_signal(barrier, inc=1, device_id=target, device_id_type=MESH)
    pl.semaphore_wait(barrier, len(targets))


def ctx_neighbours():
    e = lax.axis_index("exp")
    return [(ctx_at(STEP[t]), e) for t in "RLYS"]


class Gather:
    def __init__(self, number, mode, slot, send, recv):
        self.number, self.mode, self.slot = number, mode, slot
        self.send, self.recv = send, recv
        self.depth = []
        for trigger, _, _, _ in mode:
            self.depth.append(0 if trigger is None else self.depth[trigger] + 1)

    def copy(self, j, arriving):
        trigger, rel, half, to = self.mode[j]
        e = lax.axis_index("exp")
        at = plus(FROM[to], rel) if arriving else rel
        ref = self.slot(ctx_at(at), half)
        source = ref
        return pltpu.make_async_remote_copy(
            src_ref=source,
            dst_ref=ref,
            send_sem=self.send.at[self.number, j],
            recv_sem=self.recv.at[self.number, j],
            device_id=(ctx_at(STEP[to]), e),
            device_id_type=MESH,
        )

    def start(self, trigger):
        for j, transfer in enumerate(self.mode):
            if transfer[0] == trigger:
                self.copy(j, False).start()

    def arrive(self, j):
        self.copy(j, True).wait_recv()

    def events(self):
        triggers = sorted({t[0] for t in self.mode if t[0] is not None})
        out = [(0, functools.partial(self.start, None))]

        def forward(j):
            self.arrive(j)
            self.start(j)

        for j in triggers:
            out.append((self.depth[j] + 1, functools.partial(forward, j)))
        return out

    def finish(self):
        forwarded = {t[0] for t in self.mode}
        for j in range(len(self.mode)):
            if j not in forwarded:
                self.arrive(j)

    def drain(self):
        for j in range(len(self.mode)):
            self.copy(j, False).wait_send()


CHIPS = ((0, 0), (0, 1), (3, 0), (1, 0), (3, 1), (1, 1), (2, 1), (2, 0))
SOURCE = {1: 0, 3: 1, 2: 2}
ROWS = 64


class LocalGather(Gather):
    def copy(self, j, arriving):
        trigger, rel, half, to = self.mode[j]
        e = lax.axis_index("exp")
        there = plus(FROM[to], rel)
        here = there if arriving else plus(rel, (0, 0, 0))
        return pltpu.make_async_remote_copy(
            src_ref=self.slot(here, half),
            dst_ref=self.slot(there, half),
            send_sem=self.send.at[self.number, j],
            recv_sem=self.recv.at[self.number, j],
            device_id=(ctx_at(STEP[to]), e),
            device_id_type=MESH,
        )


def expert_kernel(
    arrived, gate, up, down, residual, mix, out,
    tok, wgu, wdn, hid, part, from_sib, x_first, y_sum, y_first, x_sum, slots, returned,
    ag_send, ag_recv, w_sem, own_sem, rs_send, rs_recv, back_send, back_recv,
):
    c, e = lax.axis_index("ctx"), lax.axis_index("exp")
    peers = [lax.rem(e + d, 8) for d in range(1, 8)]
    f32, bf16 = jnp.float32, jnp.bfloat16
    units, width = down.shape[1:]
    half_width = width // 2
    own_copy = pltpu.make_async_copy(arrived, tok.at[0, pl.ds(0, ROWS), :], own_sem)
    own_copy.start()
    loads = [
        pltpu.make_async_copy(gate.at[0], wgu.at[:, pl.ds(0, units)], w_sem.at[0]),
        pltpu.make_async_copy(up.at[0], wgu.at[:, pl.ds(units, units)], w_sem.at[1]),
        pltpu.make_async_copy(down.at[0], wdn, w_sem.at[2]),
    ]
    greet(ctx_neighbours() + [(ctx_at((2, 0, 0)), e)] + [(c, to) for to in peers])
    own_copy.wait()

    pieces = []
    for number, mode in enumerate((Y_THEN_X, X_THEN_Y)):
        rows = ROWS // 2

        def slot(rel, half, first=number * rows, rows=rows):
            g, start = CHIPS.index(rel[:2]), rel[2] * ROWS + first
            if half is None:
                return tok.at[g, pl.ds(start, rows), :]
            return tok.at[g, pl.ds(start + half * (rows // 2), rows // 2), :]

        pieces.append(LocalGather(number, mode, slot, ag_send, ag_recv))
    first, second = pieces
    second.start(None)
    first.start(None)
    for load in loads:
        load.start()

    def forward(piece, *js):
        for j in js:
            piece.arrive(j)
            piece.start(j)

    def need(piece, *js):
        for j in js:
            piece.arrive(j)

    def rs_copy(j, source, target, to):
        return pltpu.make_async_remote_copy(
            src_ref=source, dst_ref=target, send_sem=rs_send.at[j], recv_sem=rs_recv.at[j],
            device_id=(ctx_at(to), e), device_id_type=MESH,
        )

    mine = pl.ds(0, ROWS)
    lhs, rhs = pl.ds(0, half_width), pl.ds(half_width, half_width)

    def to_sib(g):
        return rs_copy(g, part.at[g, pl.ds(ROWS, ROWS), :], from_sib.at[g], (0, 0, 1))

    x_first_copy, y_first_copy, x_sum_copy = {}, {}, {}
    for g, (dx, dy) in enumerate(CHIPS):
        if dx:
            s = SOURCE[dx]
            x_first_copy[dx, dy] = rs_copy(8 + s * 2 + dy, part.at[g, mine, lhs], x_first.at[s, dy], (dx, 0, 0))
            if not dy:
                x_sum_copy[dx] = rs_copy(14 + s, part.at[g, mine, rhs], x_sum.at[s], (dx, 0, 0))
        if dy:
            y_first_copy[dx] = rs_copy(17 + dx, part.at[g, mine, rhs], y_first.at[dx], (0, 1, 0))
    y_sum_copy = rs_copy(21, part.at[1, mine, lhs], y_sum, (0, 1, 0))

    def merge(g):
        to_sib(g).wait_recv()
        part[g, mine, :] = (part[g, mine, :].astype(f32) + from_sib[g].astype(f32)).astype(bf16)

    def send(g):
        dx, dy = CHIPS[g]
        if dx:
            x_first_copy[dx, dy].start()
        if dy:
            y_first_copy[dx].start()

    def send_right(dx):
        g = CHIPS.index((dx, 0))
        y_first_copy[dx].wait_recv()
        part[g, mine, rhs] = (part[g, mine, rhs].astype(f32) + y_first[dx].astype(f32)).astype(bf16)
        if dx:
            x_sum_copy[dx].start()

    before = {
        0: lambda: (need(first, 3), need(second, 3), loads[0].wait(), loads[1].wait()),
        1: lambda: (
            forward(second, 0, 1), need(first, 6), need(second, 10), forward(first, 1, 2),
        ),
        2: lambda: (forward(second, 4, 7), need(first, 8), need(second, 6)),
        3: lambda: (forward(first, 4, 5), need(first, 10), need(second, 9)),
        4: lambda: (forward(first, 7, 9), need(first, 12), need(second, 15)),
        5: lambda: (forward(first, 11, 13), need(first, 14), need(second, 16)),
        6: lambda: (need(first, 17, 18), need(second, 17, 18)),
        7: lambda: (need(first, 15, 16), need(second, 12, 14)),
    }
    between = {
        0: lambda: (forward(first, 0), forward(second, 2), loads[2].wait()),
        3: lambda: (forward(second, 5, 8), send_right(0)),
        5: lambda: (forward(second, 11, 13),),
        6: lambda: (send_right(3),),
        7: lambda: (send_right(1),),
    }

    def at_step(g, actions):
        for at, action in actions.items():

            @pl.when(g == at)
            def _(action=action):
                action()

    def step(g, _):
        at_step(g, before)
        both = jnp.dot(tok[g], wgu[...], preferred_element_type=f32)
        v = both[:, :units]
        hid[...] = (v / (1.0 + jnp.exp(-v)) * both[:, units:]).astype(bf16)

        @pl.when(g > 0)
        def _():
            merge(g - 1)

        for at in range(1, 8):
            pl.when(g == at)(functools.partial(send, at - 1))
        at_step(g, between)
        part[g] = jnp.dot(hid[...], wdn[...], preferred_element_type=f32).astype(bf16)
        to_sib(g).start()
        return 0

    lax.fori_loop(0, 8, step, 0)
    merge(7)
    send(7)
    send_right(2)

    moves = {}

    def give_back(h, value):
        cols = rhs if h else lhs
        slots[:, :, cols] = value.reshape(8, ROWS // 8, half_width).astype(bf16)
        moves[h] = [
            pltpu.make_async_remote_copy(
                src_ref=slots.at[to, :, cols],
                dst_ref=returned.at[e, :, cols],
                send_sem=back_send.at[h, d],
                recv_sem=back_recv.at[h, d],
                device_id=(c, to),
                device_id_type=MESH,
            )
            for d, to in enumerate(peers)
        ]
        for move in moves[h]:
            move.start()
        returned[e, :, cols] = slots[e, :, cols]

    for dx in (1, 3, 2):
        x_first_copy[dx, 1].wait_recv()
    total = part[1, mine, lhs].astype(f32)
    for s in range(3):
        total = total + x_first[s, 1].astype(f32)
    part[1, mine, lhs] = total.astype(bf16)
    y_sum_copy.start()
    for dx in (1, 3, 2):
        x_sum_copy[dx].wait_recv()
    total = part[0, mine, rhs].astype(f32)
    for s in range(3):
        total = total + x_sum[s].astype(f32)
    give_back(1, total)
    for dx in (1, 3, 2):
        x_first_copy[dx, 0].wait_recv()
    total = part[0, mine, lhs].astype(f32)
    for s in range(3):
        total = total + x_first[s, 0].astype(f32)
    y_sum_copy.wait_recv()
    give_back(0, total + y_sum[...].astype(f32))
    hi = mix[...].astype(bf16)
    lo = (mix[...] - hi.astype(f32)).astype(bf16)
    for h, cols in ((1, rhs), (0, lhs)):
        for move in moves[h]:
            move.wait_recv()
        outcome = returned[:, :, cols].astype(f32).reshape(ROWS, half_width).astype(bf16)
        mixture = jnp.dot(hi, outcome, preferred_element_type=f32) + jnp.dot(lo, outcome, preferred_element_type=f32)
        out[:, cols] = (residual[:, cols].astype(f32) + mixture).astype(bf16)
    for h in range(2):
        for move in moves[h]:
            move.wait_send()
    for piece in pieces:
        piece.drain()
    for copies in (x_first_copy, y_first_copy, x_sum_copy):
        for copy in copies.values():
            copy.wait_send()
    y_sum_copy.wait_send()
    for g in range(8):
        to_sib(g).wait_send()


def experts(arrived, w_gate, w_up, w_down, residual, mix):
    rows, width = arrived.shape
    ff = w_gate.shape[2]
    bf16 = jnp.bfloat16
    return pl.pallas_call(
        expert_kernel,
        out_shape=jax.ShapeDtypeStruct(residual.shape, bf16),
        in_specs=[pl.BlockSpec(memory_space=pltpu.HBM)] * 4 + [pl.BlockSpec(memory_space=pltpu.VMEM)] * 2,
        out_specs=pl.BlockSpec(memory_space=pltpu.VMEM),
        scratch_shapes=[
            pltpu.VMEM((8, 2 * rows, width), bf16),
            pltpu.VMEM((width, 2 * ff), bf16),
            pltpu.VMEM((ff, width), bf16),
            pltpu.VMEM((2 * rows, ff), bf16),
            pltpu.VMEM((8, 2 * rows, width), bf16),
            pltpu.VMEM((8, rows, width), bf16),
            pltpu.VMEM((3, 2, rows, width // 2), bf16),
            pltpu.VMEM((rows, width // 2), bf16),
            pltpu.VMEM((4, rows, width // 2), bf16),
            pltpu.VMEM((3, rows, width // 2), bf16),
            pltpu.VMEM((8, rows // 8, width), bf16),
            pltpu.VMEM((8, rows // 8, width), bf16),
            pltpu.SemaphoreType.DMA((2, N_TRANSFERS)),
            pltpu.SemaphoreType.DMA((2, N_TRANSFERS)),
            pltpu.SemaphoreType.DMA((3,)),
            pltpu.SemaphoreType.DMA,
            pltpu.SemaphoreType.DMA((22,)),
            pltpu.SemaphoreType.DMA((22,)),
            pltpu.SemaphoreType.DMA((2, 7)),
            pltpu.SemaphoreType.DMA((2, 7)),
        ],
        compiler_params=pltpu.CompilerParams(
            collective_id=3, has_side_effects=True, vmem_limit_bytes=58 * 1024 * 1024
        ),
        name="experts",
    )(arrived, w_gate, w_up, w_down, residual, mix)


def mixer_kernel(
    hidden, attn_gain, w_query, w_key, w_value, w_out, prior_keys, prior_values, cosine, sine, ffn_gain, select,
    residual_out, arrived_out,
    normed, wkv, wq, kv, wo, query, scores, best, mass, blend, attended, part, from_exp, slots,
    send, recv, local, rs_send, rs_recv, to_send, to_recv,
):
    c, e = lax.axis_index("ctx"), lax.axis_index("exp")
    f32, bf16 = jnp.float32, jnp.bfloat16
    tokens, width = hidden.shape
    depth = w_query.shape[0]
    heads = w_query.shape[1] // HEAD_DIM
    tok_dev = residual_out.shape[0]
    out_cols = w_out.shape[1]
    span = kv.shape[0] // 2

    own_rows = pl.ds(pl.multiple_of(c * depth, depth), depth)
    own_keys = pl.ds(pl.multiple_of(c * tokens, tokens), tokens)
    left, right = pl.ds(0, HEAD_DIM), pl.ds(HEAD_DIM, HEAD_DIM)
    copies = [
        pltpu.make_async_copy(source, target, local.at[i])
        for i, (source, target) in enumerate(
            (
                (w_key, wkv.at[own_rows, left]),
                (w_value, wkv.at[own_rows, right]),
                (prior_keys, kv.at[own_keys, left]),
                (prior_values, kv.at[own_keys, right]),
                (w_query, wq.at[own_rows, :]),
                (w_out, wo.at[c]),
            )
        )
    ]
    for copy in copies:
        copy.start()
    greet(
        [(ctx_at(step), e) for step in STEP.values()] + [(c, lax.rem(e + d, 8)) for d in range(1, 8)]
    )
    for copy in copies:
        copy.wait()

    def rows_of(buffer, stride, base, first, rows):
        def slot(index, half):
            part_rows = rows if half is None else rows // 2
            start = base + index * stride + first + (0 if half is None else half * part_rows)
            return buffer.at[pl.ds(pl.multiple_of(start, 16), part_rows), :]

        return slot

    def block_of(buffer, first, rows):
        def slot(index, half):
            part_rows = rows if half is None else rows // 2
            return buffer.at[index, pl.ds(first + (0 if half is None else half * part_rows), part_rows), :]

        return slot

    plan = []
    for buffer, stride in ((wkv, depth), (kv, tokens), (wq, depth)):
        for i, mode in enumerate((Y_THEN_X, X_THEN_Y)):
            plan.append((mode, rows_of(buffer, stride, 0, i * stride // 2, stride // 2)))
    for i, mode in enumerate((Y_THEN_X, X_THEN_Y)):
        rows = w_out.shape[0] // 2
        plan.append((mode, block_of(wo, i * rows, rows)))
    pieces = [Gather(n, mode, slot, send, recv) for n, (mode, slot) in enumerate(plan)]
    now = Gather(len(pieces), DIRECT, rows_of(kv, tokens, span, 0, tokens), send, recv)

    tile = 16

    def norm_rows(i, _):
        rows = pl.ds(pl.multiple_of(i * tile, tile), tile)
        wide = hidden[rows, :].astype(f32)
        inverse = lax.rsqrt(jnp.mean(wide * wide, axis=-1, keepdims=True) + 1e-05)
        normed[rows, :] = (wide * inverse * attn_gain[...].astype(f32)).astype(bf16)
        return 0

    def normalise():
        lax.fori_loop(0, tokens // tile, norm_rows, 0)

    def turned(a):
        return (a * cosine[...] + pltpu.roll(a, HEAD_DIM // 2, 1) * sine[...]).astype(bf16)

    def keys_and_values():
        for piece in pieces[:2]:
            piece.finish()
        both = jnp.dot(normed[...], wkv[...], preferred_element_type=f32)
        rows = pl.ds(pl.multiple_of(span + c * tokens, tokens), tokens)
        kv[rows, left] = turned(both[:, :HEAD_DIM])
        kv[rows, right] = both[:, HEAD_DIM:].astype(bf16)
        now.start(None)

    def queries():
        for piece in pieces[4:6]:
            piece.finish()
        for g in range(heads):
            raw = jnp.dot(normed[...], wq[:, pl.ds(g * HEAD_DIM, HEAD_DIM)], preferred_element_type=f32)
            query[pl.ds(g * tokens, tokens), :] = turned(raw)

    count = heads * tokens
    block = 2 * tokens
    blocks = span // block
    inverse_root = 1.0 / math.sqrt(HEAD_DIM)

    def score(start, size):
        keys = kv[pl.ds(pl.multiple_of(start, tokens), size), left]
        return lax.dot_general(query[...], keys, (((1,), (1,)), ((), ())), preferred_element_type=f32) * inverse_root

    def masks():
        row = lax.broadcasted_iota(jnp.int32, (count, tokens), 0) % tokens
        col = lax.broadcasted_iota(jnp.int32, (count, tokens), 1)
        return row, col

    def all_scores():
        for piece in pieces[2:4] + [now]:
            piece.finish()
        row, col = masks()
        first = score(c * tokens, block)
        head_part = jnp.where(col > row, first[:, :tokens], -1e30)
        scores[:, pl.ds(0, tokens)] = head_part
        scores[:, pl.ds(tokens, tokens)] = first[:, tokens:]
        last = jnp.where(col <= row, score(c * tokens + span, tokens), -1e30)
        scores[:, pl.ds(span, tokens)] = last
        best[...] = jnp.maximum(jnp.maximum(head_part, first[:, tokens:]), last)

        def body(b, _):
            s = score(c * tokens + b * block, block)
            scores[:, pl.ds(pl.multiple_of(b * block, block), block)] = s
            best[...] = jnp.maximum(best[...], jnp.maximum(s[:, :tokens], s[:, tokens:]))
            return 0

        lax.fori_loop(1, blocks, body, 0)
        best[...] = jnp.broadcast_to(jnp.max(best[...], axis=1, keepdims=True), best.shape)

    def blended():
        top = best[:, pl.ds(0, 1)]
        p = jnp.exp(scores[:, pl.ds(span, tokens)] - top)
        mass[...] = p
        values = kv[pl.ds(pl.multiple_of(c * tokens + span, tokens), tokens), right]
        blend[...] = jnp.dot(p.astype(bf16), values, preferred_element_type=f32)

        def body(b, _):
            p = jnp.exp(scores[:, pl.ds(pl.multiple_of(b * block, block), block)] - top)
            mass[...] += p[:, :tokens] + p[:, tokens:]
            values = kv[pl.ds(pl.multiple_of(c * tokens + b * block, tokens), block), right]
            blend[...] += jnp.dot(p.astype(bf16), values, preferred_element_type=f32)
            return 0

        lax.fori_loop(0, blocks, body, 0)
        result = (blend[...] / jnp.sum(mass[...], axis=1, keepdims=True)).astype(bf16)
        for g in range(heads):
            attended[:, pl.ds(g * HEAD_DIM, HEAD_DIM)] = result[g * tokens:(g + 1) * tokens, :]

    def forward_now():
        for j in range(7):
            now.arrive(j)
            now.start(j)

    timeline = []
    for piece in pieces:
        for order, (level, action) in enumerate(piece.events()):
            timeline.append((piece.number + 1.0 * level, order, action))
    timeline += [
        (1.5, 0, normalise),
        (4.5, 0, keys_and_values),
        (7.5, 0, forward_now),
        (8.05, 0, queries),
        (8.1, 0, all_scores),
        (8.6, 0, blended),
    ]
    peers = [lax.rem(e + d, 8) for d in range(1, 8)]
    plane = 4 * out_cols
    shares = {}

    def project(dx, wants):
        for piece, js in zip(pieces[6:], wants):
            for j in js:
                piece.arrive(j)
        x = lax.rem(c // 4 + dx, NX)

        def one(i, _):
            index = x * 4 + i
            cols = pl.ds(pl.multiple_of(index * out_cols, out_cols), out_cols)
            part[:, cols] = jnp.dot(attended[...], wo[index], preferred_element_type=f32).astype(bf16)
            return 0

        lax.fori_loop(0, 4, one, 0)
        cols = pl.ds(pl.multiple_of(x * plane, plane), plane)
        shares[dx] = [
            pltpu.make_async_remote_copy(
                src_ref=part.at[pl.ds(pl.multiple_of(to * tok_dev, tok_dev), tok_dev), cols],
                dst_ref=from_exp.at[d, :, cols],
                send_sem=rs_send.at[dx, d],
                recv_sem=rs_recv.at[dx, d],
                device_id=(c, to),
                device_id_type=MESH,
            )
            for d, to in enumerate(peers)
        ]
        for share in shares[dx]:
            share.start()

    timeline += [
        (9.1, 0, lambda: project(0, ((3, 6), (3, 10)))),
        (9.2, 0, lambda: project(3, ((8, 12), (6, 15)))),
        (9.3, 0, lambda: project(1, ((10, 14), (9, 16)))),
        (11.0, 0, lambda: project(2, ((15, 16, 17, 18), (12, 14, 17, 18)))),
    ]
    for _, _, action in sorted(timeline, key=lambda item: item[:2]):
        action()
    for dx in (0, 3, 1, 2):
        for share in shares[dx]:
            share.wait_recv()
    mine = pl.ds(pl.multiple_of(e * tok_dev, tok_dev), tok_dev)
    total = part[mine, :].astype(f32)
    for d in range(7):
        total = total + from_exp[d].astype(f32)
    residual = (hidden[mine, :].astype(f32) + total).astype(bf16)
    residual_out[...] = residual
    wide = residual.astype(f32)
    inverse = lax.rsqrt(jnp.mean(wide * wide, axis=-1, keepdims=True) + 1e-05)
    ready = (wide * inverse * ffn_gain[...].astype(f32)).astype(bf16)
    chosen = jnp.dot(select[...], ready, preferred_element_type=f32)
    slots[...] = chosen.reshape(slots.shape).astype(bf16)
    moves = [
        pltpu.make_async_remote_copy(
            src_ref=slots.at[to],
            dst_ref=arrived_out.at[e],
            send_sem=to_send.at[d],
            recv_sem=to_recv.at[d],
            device_id=(c, to),
            device_id_type=MESH,
        )
        for d, to in enumerate(peers)
    ]
    for move in moves:
        move.start()
    arrived_out[e] = slots[e]
    for piece in pieces + [now]:
        piece.drain()
    for dx in (0, 3, 1, 2):
        for share in shares[dx]:
            share.wait_send()
    for move in moves:
        move.wait_send()
    for move in moves:
        move.wait_recv()


def mixer(hidden, attn_gain, w_query, w_key, w_value, w_out, prior_keys, prior_values, cosine, sine, ffn_gain, select):
    tokens, width = hidden.shape
    depth, q_cols = w_query.shape
    bf16, f32 = jnp.bfloat16, jnp.float32
    span = 16 * tokens
    count = q_cols // HEAD_DIM * tokens
    vmem = pl.BlockSpec(memory_space=pltpu.VMEM)
    anywhere = pl.BlockSpec(memory_space=pltpu.HBM)
    return pl.pallas_call(
        mixer_kernel,
        out_shape=[
            jax.ShapeDtypeStruct((tokens // 8, width), bf16),
            jax.ShapeDtypeStruct((8, select.shape[0] // 8, width), bf16),
        ],
        in_specs=[vmem, vmem] + [anywhere] * 6 + [vmem] * 4,
        out_specs=[vmem] * 2,
        scratch_shapes=[
            pltpu.VMEM((tokens, width), bf16),
            pltpu.VMEM((16 * depth, 2 * HEAD_DIM), bf16),
            pltpu.VMEM((16 * depth, q_cols), bf16),
            pltpu.VMEM((2 * span, 2 * HEAD_DIM), bf16),
            pltpu.VMEM((16,) + w_out.shape, bf16),
            pltpu.VMEM((count, HEAD_DIM), bf16),
            pltpu.VMEM((count, span + tokens), f32),
            pltpu.VMEM((count, tokens), f32),
            pltpu.VMEM((count, tokens), f32),
            pltpu.VMEM((count, HEAD_DIM), f32),
            pltpu.VMEM((tokens, q_cols), bf16),
            pltpu.VMEM((tokens, width), bf16),
            pltpu.VMEM((7, tokens // 8, width), bf16),
            pltpu.VMEM((8, select.shape[0] // 8, width), bf16),
            pltpu.SemaphoreType.DMA((9, N_TRANSFERS)),
            pltpu.SemaphoreType.DMA((9, N_TRANSFERS)),
            pltpu.SemaphoreType.DMA((6,)),
            pltpu.SemaphoreType.DMA((4, 7)),
            pltpu.SemaphoreType.DMA((4, 7)),
            pltpu.SemaphoreType.DMA((7,)),
            pltpu.SemaphoreType.DMA((7,)),
        ],
        compiler_params=pltpu.CompilerParams(
            collective_id=0, has_side_effects=True, vmem_limit_bytes=60 * 1024 * 1024
        ),
        name="mixer",
    )(hidden, attn_gain, w_query, w_key, w_value, w_out, prior_keys, prior_values, cosine, sine, ffn_gain, select)


def local(
    hidden_in,
    attn_gain,
    w_query,
    w_key,
    w_value,
    w_out,
    prior_keys,
    prior_values,
    stretch_offset,
    ffn_gain,
    w_gate,
    w_up,
    w_down,
    expert_ids,
    gate_weights,
):
    exp_count = lax.axis_size("exp")
    ctx_index = lax.axis_index("ctx")
    exp_index = lax.axis_index("exp")
    local_len, model_width = hidden_in.shape
    tok_dev = local_len // exp_count
    positions = stretch_offset[0] + ctx_index * local_len + jnp.arange(local_len, dtype=jnp.int32)
    half_dim = HEAD_DIM // 2
    frequency = jnp.exp(jnp.arange(half_dim).astype(jnp.float32) * (-2.0 * math.log(1000000.0) / HEAD_DIM))
    angles = positions.astype(jnp.float32)[:, None] * frequency[None, :]
    cosine, sine = jnp.cos(angles), jnp.sin(angles)
    capacity = 4 * tok_dev // exp_count
    device_row = (ctx_index * exp_count + exp_index) * tok_dev
    my_ids = lax.dynamic_slice_in_dim(expert_ids, device_row, tok_dev, 0)
    flat = my_ids.reshape(-1)
    same = flat[:, None] == flat[None, :]
    earlier = jnp.arange(2 * tok_dev)[:, None] < jnp.arange(2 * tok_dev)[None, :]
    place = flat * capacity + jnp.sum(same & earlier, axis=0, dtype=jnp.int32)
    place = place.reshape(tok_dev, 2)
    held = place[:, :, None] == jnp.arange(exp_count * capacity, dtype=jnp.int32)[None, None, :]
    select = jnp.any(held, axis=1).T.astype(jnp.bfloat16)
    mix = jnp.sum(jnp.where(held, gate_weights[:, :, None], 0.0), axis=1)
    residual, arrived = mixer(
        hidden_in,
        attn_gain[None],
        w_query,
        w_key,
        w_value,
        w_out,
        prior_keys,
        prior_values,
        jnp.concatenate([cosine, cosine], axis=1),
        jnp.concatenate([-sine, sine], axis=1),
        ffn_gain[None],
        select,
    )
    return experts(arrived.reshape(-1, model_width), w_gate, w_up, w_down, residual, mix)


def solution(mesh):
    in_specs = (
        P("ctx", None),
        P(),
        P("ctx", "exp"),
        P("ctx", "exp"),
        P("ctx", "exp"),
        P("exp", "ctx"),
        P("ctx", "exp"),
        P("ctx", "exp"),
        P(),
        P(),
        P("exp", None, "ctx"),
        P("exp", None, "ctx"),
        P("exp", "ctx", None),
        P(),
        P(("ctx", "exp"), None),
    )
    out_specs = P(("ctx", "exp"), None)
    return jax.shard_map(local, mesh=mesh, in_specs=in_specs, out_specs=out_specs, check_vma=False)
```

```python
import functools
import math

import jax
import jax.numpy as jnp
from jax import lax
from jax.experimental import pallas as pl
from jax.experimental.pallas import tpu as pltpu
from jax.sharding import PartitionSpec as P

HEADS = 32
KV_HEADS = 8
HEAD_DIM = 128
MESH = pl.DeviceIdType.MESH
NX, NY, NK = 4, 2, 2

Y_THEN_X = (
    (None, (0, 0, 0), None, "Y"),
    (None, (0, 0, 0), None, "R"),
    (None, (0, 0, 0), None, "L"),
    (None, (0, 0, 0), None, "S"),
    (0, (0, 1, 0), None, "R"),
    (0, (0, 1, 0), None, "L"),
    (0, (0, 1, 0), None, "S"),
    (1, (-1, 0, 0), 0, "R"),
    (1, (-1, 0, 0), None, "S"),
    (2, (1, 0, 0), 1, "L"),
    (2, (1, 0, 0), None, "S"),
    (4, (-1, 1, 0), 0, "R"),
    (4, (-1, 1, 0), None, "S"),
    (5, (1, 1, 0), 1, "L"),
    (5, (1, 1, 0), None, "S"),
    (7, (2, 0, 0), 0, "S"),
    (9, (2, 0, 0), 1, "S"),
    (11, (2, 1, 0), 0, "S"),
    (13, (2, 1, 0), 1, "S"),
)
X_THEN_Y = (
    (None, (0, 0, 0), None, "R"),
    (None, (0, 0, 0), None, "L"),
    (None, (0, 0, 0), None, "Y"),
    (None, (0, 0, 0), None, "S"),
    (0, (-1, 0, 0), 0, "R"),
    (0, (-1, 0, 0), None, "Y"),
    (0, (-1, 0, 0), None, "S"),
    (1, (1, 0, 0), 1, "L"),
    (1, (1, 0, 0), None, "Y"),
    (1, (1, 0, 0), None, "S"),
    (2, (0, 1, 0), None, "S"),
    (4, (2, 0, 0), 0, "Y"),
    (4, (2, 0, 0), 0, "S"),
    (7, (2, 0, 0), 1, "Y"),
    (7, (2, 0, 0), 1, "S"),
    (5, (-1, 1, 0), None, "S"),
    (8, (1, 1, 0), None, "S"),
    (11, (2, 1, 0), 0, "S"),
    (13, (2, 1, 0), 1, "S"),
)
DIRECT = tuple((None, (0, 0, 0), None, to) for to in ("R", "L", "Y", "O", "RY", "LY", "OY", "S")) + (
    (0, (-1, 0, 0), None, "S"),
    (1, (1, 0, 0), None, "S"),
    (2, (0, 1, 0), None, "S"),
    (3, (2, 0, 0), None, "S"),
    (4, (-1, 1, 0), None, "S"),
    (5, (1, 1, 0), None, "S"),
    (6, (2, 1, 0), None, "S"),
)
N_TRANSFERS = 19
STEP = {
    "R": (1, 0, 0), "L": (-1, 0, 0), "Y": (0, 1, 0), "S": (0, 0, 1),
    "O": (2, 0, 0), "RY": (1, 1, 0), "LY": (-1, 1, 0), "OY": (2, 1, 0),
}
FROM = {to: (-step[0], step[1], step[2]) for to, step in STEP.items()}


def ctx_at(delta):
    c = lax.axis_index("ctx")
    x = (c // 4 + delta[0] + NX) % NX
    y = ((c // 2) % 2 + delta[1]) % NY
    k = (c % 2 + delta[2]) % NK
    return x * 4 + y * 2 + k


def plus(a, b):
    return ((a[0] + b[0]) % NX, (a[1] + b[1]) % NY, (a[2] + b[2]) % NK)


def greet(targets):
    barrier = pltpu.get_barrier_semaphore()
    for target in targets:
        pl.semaphore_signal(barrier, inc=1, device_id=target, device_id_type=MESH)
    pl.semaphore_wait(barrier, len(targets))


def ctx_neighbours():
    e = lax.axis_index("exp")
    return [(ctx_at(STEP[t]), e) for t in "RLYS"]


class Gather:
    def __init__(self, number, mode, slot, send, recv):
        self.number, self.mode, self.slot = number, mode, slot
        self.send, self.recv = send, recv
        self.depth = []
        for trigger, _, _, _ in mode:
            self.depth.append(0 if trigger is None else self.depth[trigger] + 1)

    def copy(self, j, arriving):
        trigger, rel, half, to = self.mode[j]
        e = lax.axis_index("exp")
        at = plus(FROM[to], rel) if arriving else rel
        ref = self.slot(ctx_at(at), half)
        source = ref
        return pltpu.make_async_remote_copy(
            src_ref=source,
            dst_ref=ref,
            send_sem=self.send.at[self.number, j],
            recv_sem=self.recv.at[self.number, j],
            device_id=(ctx_at(STEP[to]), e),
            device_id_type=MESH,
        )

    def start(self, trigger):
        for j, transfer in enumerate(self.mode):
            if transfer[0] == trigger:
                self.copy(j, False).start()

    def arrive(self, j):
        self.copy(j, True).wait_recv()

    def events(self):
        triggers = sorted({t[0] for t in self.mode if t[0] is not None})
        out = [(0, functools.partial(self.start, None))]

        def forward(j):
            self.arrive(j)
            self.start(j)

        for j in triggers:
            out.append((self.depth[j] + 1, functools.partial(forward, j)))
        return out

    def finish(self):
        forwarded = {t[0] for t in self.mode}
        for j in range(len(self.mode)):
            if j not in forwarded:
                self.arrive(j)

    def drain(self):
        for j in range(len(self.mode)):
            self.copy(j, False).wait_send()


CHIPS = ((0, 0), (0, 1), (3, 0), (1, 0), (3, 1), (1, 1), (2, 1), (2, 0))
SOURCE = {1: 0, 3: 1, 2: 2}
ROWS = 64
PIECES = ((X_THEN_Y, 16), (Y_THEN_X, 48))


class LocalGather(Gather):
    def copy(self, j, arriving):
        trigger, rel, half, to = self.mode[j]
        e = lax.axis_index("exp")
        there = plus(FROM[to], rel)
        here = there if arriving else plus(rel, (0, 0, 0))
        return pltpu.make_async_remote_copy(
            src_ref=self.slot(here, half),
            dst_ref=self.slot(there, half),
            send_sem=self.send.at[self.number, j],
            recv_sem=self.recv.at[self.number, j],
            device_id=(ctx_at(STEP[to]), e),
            device_id_type=MESH,
        )


def expert_kernel(
    arrived, gate, up, down, residual, mix, out,
    tok, wgu, wdn, hid, part, from_sib, x_first, y_sum, y_first, x_sum, slots, returned,
    ag_send, ag_recv, w_sem, own_sem, rs_send, rs_recv, back_send, back_recv,
):
    c, e = lax.axis_index("ctx"), lax.axis_index("exp")
    peers = [lax.rem(e + d, 8) for d in range(1, 8)]
    f32, bf16 = jnp.float32, jnp.bfloat16
    units, width = down.shape[1:]
    half_width = width // 2
    own_copy = pltpu.make_async_copy(arrived, tok.at[0, pl.ds(0, ROWS), :], own_sem)
    own_copy.start()
    loads = [
        pltpu.make_async_copy(gate.at[0], wgu.at[:, pl.ds(0, units)], w_sem.at[0]),
        pltpu.make_async_copy(up.at[0], wgu.at[:, pl.ds(units, units)], w_sem.at[1]),
        pltpu.make_async_copy(down.at[0], wdn, w_sem.at[2]),
    ]
    greet(ctx_neighbours() + [(ctx_at((2, 0, 0)), e)] + [(c, to) for to in peers])
    own_copy.wait()

    pieces, first, second, begin = [], [], [], 0
    for number, (mode, rows) in enumerate(PIECES):

        def slot(rel, half, begin=begin, rows=rows):
            g, start = CHIPS.index(rel[:2]), rel[2] * ROWS + begin
            if half is None:
                return tok.at[g, pl.ds(start, rows), :]
            return tok.at[g, pl.ds(start, rows), pl.ds(half * half_width, half_width)]

        pieces.append(LocalGather(number, mode, slot, ag_send, ag_recv))
        (first if mode is Y_THEN_X else second).append(pieces[-1])
        begin += rows
    for piece in pieces:
        piece.start(None)
    for load in loads:
        load.start()

    def forward(group, *js):
        for j in js:
            for piece in group:
                piece.arrive(j)
                piece.start(j)

    def need(group, *js):
        for j in js:
            for piece in group:
                piece.arrive(j)

    def rs_copy(j, source, target, to):
        return pltpu.make_async_remote_copy(
            src_ref=source, dst_ref=target, send_sem=rs_send.at[j], recv_sem=rs_recv.at[j],
            device_id=(ctx_at(to), e), device_id_type=MESH,
        )

    mine = pl.ds(0, ROWS)
    lhs, rhs = pl.ds(0, half_width), pl.ds(half_width, half_width)

    def to_sib(g):
        return rs_copy(g, part.at[g, pl.ds(ROWS, ROWS), :], from_sib.at[g], (0, 0, 1))

    x_first_copy, y_first_copy, x_sum_copy = {}, {}, {}
    for g, (dx, dy) in enumerate(CHIPS):
        if dx:
            s = SOURCE[dx]
            x_first_copy[dx, dy] = rs_copy(8 + s * 2 + dy, part.at[g, mine, lhs], x_first.at[s, dy], (dx, 0, 0))
            if not dy:
                x_sum_copy[dx] = rs_copy(14 + s, part.at[g, mine, rhs], x_sum.at[s], (dx, 0, 0))
        if dy:
            y_first_copy[dx] = rs_copy(17 + dx, part.at[g, mine, rhs], y_first.at[dx], (0, 1, 0))
    y_sum_copy = rs_copy(21, part.at[1, mine, lhs], y_sum, (0, 1, 0))

    def merge(g):
        to_sib(g).wait_recv()
        part[g, mine, :] = (part[g, mine, :].astype(f32) + from_sib[g].astype(f32)).astype(bf16)

    def send(g):
        dx, dy = CHIPS[g]
        if dx:
            x_first_copy[dx, dy].start()
        if dy:
            y_first_copy[dx].start()

    def send_right(dx):
        g = CHIPS.index((dx, 0))
        y_first_copy[dx].wait_recv()
        part[g, mine, rhs] = (part[g, mine, rhs].astype(f32) + y_first[dx].astype(f32)).astype(bf16)
        if dx:
            x_sum_copy[dx].start()

    before = {
        0: lambda: (
            forward(second, 2), forward(first, 0), need(first, 3), need(second, 3), loads[0].wait(), loads[1].wait(),
        ),
        1: lambda: (
            need(first, 6), need(second, 10), forward(first, 1, 2),
        ),
        2: lambda: (forward(second, 4, 7), need(first, 8), need(second, 6)),
        3: lambda: (forward(first, 4, 5), need(first, 10), need(second, 9)),
        4: lambda: (forward(first, 7, 9), need(first, 12), need(second, 15)),
        5: lambda: (forward(first, 11, 13), need(first, 14), need(second, 16)),
        6: lambda: (need(first, 17, 18), need(second, 17, 18)),
        7: lambda: (need(first, 15, 16), need(second, 12, 14)),
    }
    between = {
        0: lambda: (forward(second, 0, 1), loads[2].wait()),
        3: lambda: (forward(second, 5, 8), send_right(0)),
        5: lambda: (forward(second, 11, 13),),
        6: lambda: (send_right(3),),
        7: lambda: (send_right(1),),
    }

    def at_step(g, actions):
        for at, action in actions.items():

            @pl.when(g == at)
            def _(action=action):
                action()

    def step(g, _):
        at_step(g, before)
        both = jnp.dot(tok[g], wgu[...], preferred_element_type=f32)
        v = both[:, :units]
        hid[...] = (v / (1.0 + jnp.exp(-v)) * both[:, units:]).astype(bf16)

        @pl.when(g > 0)
        def _():
            merge(g - 1)

        for at in range(1, 8):
            pl.when(g == at)(functools.partial(send, at - 1))
        at_step(g, between)
        part[g] = jnp.dot(hid[...], wdn[...], preferred_element_type=f32).astype(bf16)
        to_sib(g).start()
        return 0

    lax.fori_loop(0, 8, step, 0)
    merge(7)
    send(7)
    send_right(2)

    moves = {}

    def give_back(h, value):
        cols = rhs if h else lhs
        slots[:, :, cols] = value.reshape(8, ROWS // 8, half_width).astype(bf16)
        moves[h] = [
            pltpu.make_async_remote_copy(
                src_ref=slots.at[to, :, cols],
                dst_ref=returned.at[e, :, cols],
                send_sem=back_send.at[h, d],
                recv_sem=back_recv.at[h, d],
                device_id=(c, to),
                device_id_type=MESH,
            )
            for d, to in enumerate(peers)
        ]
        for move in moves[h]:
            move.start()
        returned[e, :, cols] = slots[e, :, cols]

    for dx in (1, 3, 2):
        x_first_copy[dx, 1].wait_recv()
    total = part[1, mine, lhs].astype(f32)
    for s in range(3):
        total = total + x_first[s, 1].astype(f32)
    part[1, mine, lhs] = total.astype(bf16)
    y_sum_copy.start()
    for dx in (1, 3, 2):
        x_sum_copy[dx].wait_recv()
    total = part[0, mine, rhs].astype(f32)
    for s in range(3):
        total = total + x_sum[s].astype(f32)
    give_back(1, total)
    for dx in (1, 3, 2):
        x_first_copy[dx, 0].wait_recv()
    total = part[0, mine, lhs].astype(f32)
    for s in range(3):
        total = total + x_first[s, 0].astype(f32)
    y_sum_copy.wait_recv()
    give_back(0, total + y_sum[...].astype(f32))
    hi = mix[...].astype(bf16)
    lo = (mix[...] - hi.astype(f32)).astype(bf16)
    for h, cols in ((1, rhs), (0, lhs)):
        for move in moves[h]:
            move.wait_recv()
        outcome = returned[:, :, cols].astype(f32).reshape(ROWS, half_width).astype(bf16)
        mixture = jnp.dot(hi, outcome, preferred_element_type=f32) + jnp.dot(lo, outcome, preferred_element_type=f32)
        out[:, cols] = (residual[:, cols].astype(f32) + mixture).astype(bf16)
    for h in range(2):
        for move in moves[h]:
            move.wait_send()
    for piece in pieces:
        piece.drain()
    for copies in (x_first_copy, y_first_copy, x_sum_copy):
        for copy in copies.values():
            copy.wait_send()
    y_sum_copy.wait_send()
    for g in range(8):
        to_sib(g).wait_send()


def experts(arrived, w_gate, w_up, w_down, residual, mix):
    rows, width = arrived.shape
    ff = w_gate.shape[2]
    bf16 = jnp.bfloat16
    return pl.pallas_call(
        expert_kernel,
        out_shape=jax.ShapeDtypeStruct(residual.shape, bf16),
        in_specs=[pl.BlockSpec(memory_space=pltpu.HBM)] * 4 + [pl.BlockSpec(memory_space=pltpu.VMEM)] * 2,
        out_specs=pl.BlockSpec(memory_space=pltpu.VMEM),
        scratch_shapes=[
            pltpu.VMEM((8, 2 * rows, width), bf16),
            pltpu.VMEM((width, 2 * ff), bf16),
            pltpu.VMEM((ff, width), bf16),
            pltpu.VMEM((2 * rows, ff), bf16),
            pltpu.VMEM((8, 2 * rows, width), bf16),
            pltpu.VMEM((8, rows, width), bf16),
            pltpu.VMEM((3, 2, rows, width // 2), bf16),
            pltpu.VMEM((rows, width // 2), bf16),
            pltpu.VMEM((4, rows, width // 2), bf16),
            pltpu.VMEM((3, rows, width // 2), bf16),
            pltpu.VMEM((8, rows // 8, width), bf16),
            pltpu.VMEM((8, rows // 8, width), bf16),
            pltpu.SemaphoreType.DMA((len(PIECES), N_TRANSFERS)),
            pltpu.SemaphoreType.DMA((len(PIECES), N_TRANSFERS)),
            pltpu.SemaphoreType.DMA((3,)),
            pltpu.SemaphoreType.DMA,
            pltpu.SemaphoreType.DMA((22,)),
            pltpu.SemaphoreType.DMA((22,)),
            pltpu.SemaphoreType.DMA((2, 7)),
            pltpu.SemaphoreType.DMA((2, 7)),
        ],
        compiler_params=pltpu.CompilerParams(
            collective_id=3, has_side_effects=True, vmem_limit_bytes=58 * 1024 * 1024
        ),
        name="experts",
    )(arrived, w_gate, w_up, w_down, residual, mix)


def mixer_kernel(
    hidden, attn_gain, w_query, w_key, w_value, w_out, prior_keys, prior_values, cosine, sine, ffn_gain, select,
    residual_out, arrived_out,
    normed, wkv, wq, kv, wo, query, scores, best, mass, blend, attended, part, from_exp, slots,
    send, recv, local, rs_send, rs_recv, to_send, to_recv,
):
    c, e = lax.axis_index("ctx"), lax.axis_index("exp")
    f32, bf16 = jnp.float32, jnp.bfloat16
    tokens, width = hidden.shape
    depth = w_query.shape[0]
    heads = w_query.shape[1] // HEAD_DIM
    tok_dev = residual_out.shape[0]
    out_cols = w_out.shape[1]
    span = kv.shape[0] // 2

    own_rows = pl.ds(pl.multiple_of(c * depth, depth), depth)
    own_keys = pl.ds(pl.multiple_of(c * tokens, tokens), tokens)
    left, right = pl.ds(0, HEAD_DIM), pl.ds(HEAD_DIM, HEAD_DIM)
    copies = [
        pltpu.make_async_copy(source, target, local.at[i])
        for i, (source, target) in enumerate(
            (
                (w_key, wkv.at[own_rows, left]),
                (w_value, wkv.at[own_rows, right]),
                (prior_keys, kv.at[own_keys, left]),
                (prior_values, kv.at[own_keys, right]),
                (w_query, wq.at[own_rows, :]),
                (w_out, wo.at[:, pl.ds(pl.multiple_of(c * out_cols, out_cols), out_cols)]),
            )
        )
    ]
    for copy in copies:
        copy.start()
    greet(
        [(ctx_at(step), e) for step in STEP.values()] + [(c, lax.rem(e + d, 8)) for d in range(1, 8)]
    )
    for copy in copies:
        copy.wait()

    def rows_of(buffer, stride, base, first, rows):
        def slot(index, half):
            part_rows = rows if half is None else rows // 2
            start = base + index * stride + first + (0 if half is None else half * part_rows)
            return buffer.at[pl.ds(pl.multiple_of(start, 16), part_rows), :]

        return slot

    def block_of(buffer, first, rows):
        def slot(index, half):
            part_rows = rows if half is None else rows // 2
            return buffer.at[
                pl.ds(first + (0 if half is None else half * part_rows), part_rows),
                pl.ds(pl.multiple_of(index * out_cols, out_cols), out_cols),
            ]

        return slot

    plan = []
    for buffer, stride in ((wkv, depth), (kv, tokens), (wq, depth)):
        for i, mode in enumerate((Y_THEN_X, X_THEN_Y)):
            plan.append((mode, rows_of(buffer, stride, 0, i * stride // 2, stride // 2)))
    for i, mode in enumerate((Y_THEN_X, X_THEN_Y)):
        rows = w_out.shape[0] // 2
        plan.append((mode, block_of(wo, i * rows, rows)))
    pieces = [Gather(n, mode, slot, send, recv) for n, (mode, slot) in enumerate(plan)]
    now = Gather(len(pieces), DIRECT, rows_of(kv, tokens, span, 0, tokens), send, recv)

    tile = 16

    def norm_rows(i, _):
        rows = pl.ds(pl.multiple_of(i * tile, tile), tile)
        wide = hidden[rows, :].astype(f32)
        inverse = lax.rsqrt(jnp.mean(wide * wide, axis=-1, keepdims=True) + 1e-05)
        normed[rows, :] = (wide * inverse * attn_gain[...].astype(f32)[None]).astype(bf16)
        return 0

    def normalise():
        lax.fori_loop(0, tokens // tile, norm_rows, 0)

    def turned(a):
        return (a * cosine[...] + pltpu.roll(a, HEAD_DIM // 2, 1) * sine[...]).astype(bf16)

    def keys_and_values():
        for piece in pieces[:2]:
            piece.finish()
        both = jnp.dot(normed[...], wkv[...], preferred_element_type=f32)
        rows = pl.ds(pl.multiple_of(span + c * tokens, tokens), tokens)
        kv[rows, left] = turned(both[:, :HEAD_DIM])
        kv[rows, right] = both[:, HEAD_DIM:].astype(bf16)
        now.start(None)

    def queries():
        for piece in pieces[4:6]:
            piece.finish()
        raw = jnp.dot(normed[...], wq[...], preferred_element_type=f32)
        for g in range(heads):
            query[pl.ds(g * tokens, tokens), :] = turned(raw[:, g * HEAD_DIM:(g + 1) * HEAD_DIM])

    count = heads * tokens
    block = 2 * tokens
    blocks = span // block
    inverse_root = 1.0 / math.sqrt(HEAD_DIM)

    def score(start, size):
        keys = kv[pl.ds(pl.multiple_of(start, tokens), size), left]
        return lax.dot_general(query[...], keys, (((1,), (1,)), ((), ())), preferred_element_type=f32) * inverse_root

    def masks():
        row = lax.broadcasted_iota(jnp.int32, (count, tokens), 0) % tokens
        col = lax.broadcasted_iota(jnp.int32, (count, tokens), 1)
        return row, col

    def all_scores():
        for piece in pieces[2:4] + [now]:
            piece.finish()
        row, col = masks()
        first = score(c * tokens, block)
        head_part = jnp.where(col > row, first[:, :tokens], -1e30)
        scores[:, pl.ds(0, tokens)] = head_part
        scores[:, pl.ds(tokens, tokens)] = first[:, tokens:]
        last = jnp.where(col <= row, score(c * tokens + span, tokens), -1e30)
        scores[:, pl.ds(span, tokens)] = last
        best[...] = jnp.maximum(jnp.maximum(head_part, first[:, tokens:]), last)

        def body(b, _):
            s = score(c * tokens + b * block, block)
            scores[:, pl.ds(pl.multiple_of(b * block, block), block)] = s
            best[...] = jnp.maximum(best[...], jnp.maximum(s[:, :tokens], s[:, tokens:]))
            return 0

        lax.fori_loop(1, blocks, body, 0)
        best[...] = jnp.broadcast_to(jnp.max(best[...], axis=1, keepdims=True), best.shape)

    def blended():
        top = best[:, pl.ds(0, 1)]
        p = jnp.exp(scores[:, pl.ds(span, tokens)] - top)
        mass[...] = p
        values = kv[pl.ds(pl.multiple_of(c * tokens + span, tokens), tokens), right]
        blend[...] = jnp.dot(p.astype(bf16), values, preferred_element_type=f32)

        def body(b, _):
            p = jnp.exp(scores[:, pl.ds(pl.multiple_of(b * block, block), block)] - top)
            mass[...] += p[:, :tokens] + p[:, tokens:]
            values = kv[pl.ds(pl.multiple_of(c * tokens + b * block, tokens), block), right]
            blend[...] += jnp.dot(p.astype(bf16), values, preferred_element_type=f32)
            return 0

        lax.fori_loop(0, blocks, body, 0)
        result = (blend[...] / jnp.sum(mass[...], axis=1, keepdims=True)).astype(bf16)
        for g in range(heads):
            attended[:, pl.ds(g * HEAD_DIM, HEAD_DIM)] = result[g * tokens:(g + 1) * tokens, :]

    def forward_now():
        for j in range(7):
            now.arrive(j)
            now.start(j)

    timeline = []
    for piece in pieces:
        for order, (level, action) in enumerate(piece.events()):
            timeline.append((piece.number + 1.0 * level, order, action))
    timeline += [
        (1.5, 0, normalise),
        (4.5, 0, keys_and_values),
        (7.5, 0, forward_now),
        (8.05, 0, queries),
        (8.1, 0, all_scores),
        (8.6, 0, blended),
    ]
    peers = [lax.rem(e + d, 8) for d in range(1, 8)]
    plane = 4 * out_cols
    shares = {}

    def project(dx, wants):
        for piece, js in zip(pieces[6:], wants):
            for j in js:
                piece.arrive(j)
        x = lax.rem(c // 4 + dx, NX)

        cols = pl.ds(pl.multiple_of(x * plane, plane), plane)
        part[:, cols] = jnp.dot(attended[...], wo[:, cols], preferred_element_type=f32).astype(bf16)
        shares[dx] = [
            pltpu.make_async_remote_copy(
                src_ref=part.at[pl.ds(pl.multiple_of(to * tok_dev, tok_dev), tok_dev), cols],
                dst_ref=from_exp.at[d, :, cols],
                send_sem=rs_send.at[dx, d],
                recv_sem=rs_recv.at[dx, d],
                device_id=(c, to),
                device_id_type=MESH,
            )
            for d, to in enumerate(peers)
        ]
        for share in shares[dx]:
            share.start()

    timeline += [
        (9.1, 0, lambda: project(0, ((3, 6), (3, 10)))),
        (9.2, 0, lambda: project(3, ((8, 12), (6, 15)))),
        (9.3, 0, lambda: project(1, ((10, 14), (9, 16)))),
        (11.0, 0, lambda: project(2, ((15, 16, 17, 18), (12, 14, 17, 18)))),
    ]
    for _, _, action in sorted(timeline, key=lambda item: item[:2]):
        action()
    for dx in (0, 3, 1, 2):
        for share in shares[dx]:
            share.wait_recv()
    mine = pl.ds(pl.multiple_of(e * tok_dev, tok_dev), tok_dev)
    total = part[mine, :].astype(f32)
    for d in range(7):
        total = total + from_exp[d].astype(f32)
    residual = (hidden[mine, :].astype(f32) + total).astype(bf16)
    residual_out[...] = residual
    wide = residual.astype(f32)
    inverse = lax.rsqrt(jnp.mean(wide * wide, axis=-1, keepdims=True) + 1e-05)
    ready = (wide * inverse * ffn_gain[...].astype(f32)[None]).astype(bf16)
    chosen = jnp.dot(select[...], ready, preferred_element_type=f32)
    slots[...] = chosen.reshape(slots.shape).astype(bf16)
    moves = [
        pltpu.make_async_remote_copy(
            src_ref=slots.at[to],
            dst_ref=arrived_out.at[e],
            send_sem=to_send.at[d],
            recv_sem=to_recv.at[d],
            device_id=(c, to),
            device_id_type=MESH,
        )
        for d, to in enumerate(peers)
    ]
    for move in moves:
        move.start()
    arrived_out[e] = slots[e]
    for piece in pieces + [now]:
        piece.drain()
    for dx in (0, 3, 1, 2):
        for share in shares[dx]:
            share.wait_send()
    for move in moves:
        move.wait_send()
    for move in moves:
        move.wait_recv()


def mixer(hidden, attn_gain, w_query, w_key, w_value, w_out, prior_keys, prior_values, cosine, sine, ffn_gain, select):
    tokens, width = hidden.shape
    depth, q_cols = w_query.shape
    bf16, f32 = jnp.bfloat16, jnp.float32
    span = 16 * tokens
    count = q_cols // HEAD_DIM * tokens
    vmem = pl.BlockSpec(memory_space=pltpu.VMEM)
    anywhere = pl.BlockSpec(memory_space=pltpu.HBM)
    return pl.pallas_call(
        mixer_kernel,
        out_shape=[
            jax.ShapeDtypeStruct((tokens // 8, width), bf16),
            jax.ShapeDtypeStruct((8, select.shape[0] // 8, width), bf16),
        ],
        in_specs=[vmem, vmem] + [anywhere] * 6 + [vmem] * 4,
        out_specs=[vmem] * 2,
        scratch_shapes=[
            pltpu.VMEM((tokens, width), bf16),
            pltpu.VMEM((16 * depth, 2 * HEAD_DIM), bf16),
            pltpu.VMEM((16 * depth, q_cols), bf16),
            pltpu.VMEM((2 * span, 2 * HEAD_DIM), bf16),
            pltpu.VMEM((w_out.shape[0], width), bf16),
            pltpu.VMEM((count, HEAD_DIM), bf16),
            pltpu.VMEM((count, span + tokens), f32),
            pltpu.VMEM((count, tokens), f32),
            pltpu.VMEM((count, tokens), f32),
            pltpu.VMEM((count, HEAD_DIM), f32),
            pltpu.VMEM((tokens, q_cols), bf16),
            pltpu.VMEM((tokens, width), bf16),
            pltpu.VMEM((7, tokens // 8, width), bf16),
            pltpu.VMEM((8, select.shape[0] // 8, width), bf16),
            pltpu.SemaphoreType.DMA((9, N_TRANSFERS)),
            pltpu.SemaphoreType.DMA((9, N_TRANSFERS)),
            pltpu.SemaphoreType.DMA((6,)),
            pltpu.SemaphoreType.DMA((4, 7)),
            pltpu.SemaphoreType.DMA((4, 7)),
            pltpu.SemaphoreType.DMA((7,)),
            pltpu.SemaphoreType.DMA((7,)),
        ],
        compiler_params=pltpu.CompilerParams(
            collective_id=0, has_side_effects=True, vmem_limit_bytes=60 * 1024 * 1024
        ),
        name="mixer",
    )(hidden, attn_gain, w_query, w_key, w_value, w_out, prior_keys, prior_values, cosine, sine, ffn_gain, select)


def local(
    hidden_in,
    attn_gain,
    w_query,
    w_key,
    w_value,
    w_out,
    prior_keys,
    prior_values,
    stretch_offset,
    ffn_gain,
    w_gate,
    w_up,
    w_down,
    expert_ids,
    gate_weights,
):
    exp_count = lax.axis_size("exp")
    ctx_index = lax.axis_index("ctx")
    exp_index = lax.axis_index("exp")
    local_len, model_width = hidden_in.shape
    tok_dev = local_len // exp_count
    positions = stretch_offset[0] + ctx_index * local_len + jnp.arange(local_len, dtype=jnp.int32)
    half_dim = HEAD_DIM // 2
    frequency = jnp.exp(jnp.arange(half_dim).astype(jnp.float32) * (-2.0 * math.log(1000000.0) / HEAD_DIM))
    angles = positions.astype(jnp.float32)[:, None] * frequency[None, :]
    cosine, sine = jnp.cos(angles), jnp.sin(angles)
    capacity = 4 * tok_dev // exp_count
    device_row = (ctx_index * exp_count + exp_index) * tok_dev
    my_ids = lax.dynamic_slice_in_dim(expert_ids, device_row, tok_dev, 0)
    flat = my_ids.reshape(-1)
    same = flat[:, None] == flat[None, :]
    earlier = jnp.arange(2 * tok_dev)[:, None] < jnp.arange(2 * tok_dev)[None, :]
    place = flat * capacity + jnp.sum(same & earlier, axis=0, dtype=jnp.int32)
    place = place.reshape(tok_dev, 2)
    held = place[:, :, None] == jnp.arange(exp_count * capacity, dtype=jnp.int32)[None, None, :]
    select = jnp.any(held, axis=1).T.astype(jnp.bfloat16)
    mix = jnp.sum(jnp.where(held, gate_weights[:, :, None], 0.0), axis=1)
    residual, arrived = mixer(
        hidden_in,
        attn_gain,
        w_query,
        w_key,
        w_value,
        w_out,
        prior_keys,
        prior_values,
        jnp.concatenate([cosine, cosine], axis=1),
        jnp.concatenate([-sine, sine], axis=1),
        ffn_gain,
        select,
    )
    return experts(arrived.reshape(-1, model_width), w_gate, w_up, w_down, residual, mix)


def solution(mesh):
    in_specs = (
        P("ctx", None),
        P(),
        P("ctx", "exp"),
        P("ctx", "exp"),
        P("ctx", "exp"),
        P("exp", "ctx"),
        P("ctx", "exp"),
        P("ctx", "exp"),
        P(),
        P(),
        P("exp", None, "ctx"),
        P("exp", None, "ctx"),
        P("exp", "ctx", None),
        P(),
        P(("ctx", "exp"), None),
    )
    out_specs = P(("ctx", "exp"), None)
    return jax.shard_map(local, mesh=mesh, in_specs=in_specs, out_specs=out_specs, check_vma=False)
```

```python
import functools
import math

import jax
import jax.numpy as jnp
from jax import lax
from jax.experimental import pallas as pl
from jax.experimental.pallas import tpu as pltpu
from jax.sharding import PartitionSpec as P

HEADS = 32
KV_HEADS = 8
HEAD_DIM = 128
MESH = pl.DeviceIdType.MESH
NX, NY, NK = 4, 2, 2

Y_THEN_X = (
    (None, (0, 0, 0), None, "Y"),
    (None, (0, 0, 0), None, "R"),
    (None, (0, 0, 0), None, "L"),
    (None, (0, 0, 0), None, "S"),
    (0, (0, 1, 0), None, "R"),
    (0, (0, 1, 0), None, "L"),
    (0, (0, 1, 0), None, "S"),
    (1, (-1, 0, 0), 0, "R"),
    (1, (-1, 0, 0), None, "S"),
    (2, (1, 0, 0), 1, "L"),
    (2, (1, 0, 0), None, "S"),
    (4, (-1, 1, 0), 0, "R"),
    (4, (-1, 1, 0), None, "S"),
    (5, (1, 1, 0), 1, "L"),
    (5, (1, 1, 0), None, "S"),
    (7, (2, 0, 0), 0, "S"),
    (9, (2, 0, 0), 1, "S"),
    (11, (2, 1, 0), 0, "S"),
    (13, (2, 1, 0), 1, "S"),
)
X_THEN_Y = (
    (None, (0, 0, 0), None, "R"),
    (None, (0, 0, 0), None, "L"),
    (None, (0, 0, 0), None, "Y"),
    (None, (0, 0, 0), None, "S"),
    (0, (-1, 0, 0), 0, "R"),
    (0, (-1, 0, 0), None, "Y"),
    (0, (-1, 0, 0), None, "S"),
    (1, (1, 0, 0), 1, "L"),
    (1, (1, 0, 0), None, "Y"),
    (1, (1, 0, 0), None, "S"),
    (2, (0, 1, 0), None, "S"),
    (4, (2, 0, 0), 0, "Y"),
    (4, (2, 0, 0), 0, "S"),
    (7, (2, 0, 0), 1, "Y"),
    (7, (2, 0, 0), 1, "S"),
    (5, (-1, 1, 0), None, "S"),
    (8, (1, 1, 0), None, "S"),
    (11, (2, 1, 0), 0, "S"),
    (13, (2, 1, 0), 1, "S"),
)
DIRECT = tuple((None, (0, 0, 0), None, to) for to in ("R", "L", "Y", "O", "RY", "LY", "OY", "S")) + (
    (0, (-1, 0, 0), None, "S"),
    (1, (1, 0, 0), None, "S"),
    (2, (0, 1, 0), None, "S"),
    (3, (2, 0, 0), None, "S"),
    (4, (-1, 1, 0), None, "S"),
    (5, (1, 1, 0), None, "S"),
    (6, (2, 1, 0), None, "S"),
)
N_TRANSFERS = 19
STEP = {
    "R": (1, 0, 0), "L": (-1, 0, 0), "Y": (0, 1, 0), "S": (0, 0, 1),
    "O": (2, 0, 0), "RY": (1, 1, 0), "LY": (-1, 1, 0), "OY": (2, 1, 0),
}
FROM = {to: (-step[0], step[1], step[2]) for to, step in STEP.items()}


def ctx_at(delta):
    c = lax.axis_index("ctx")
    x = (c // 4 + delta[0] + NX) % NX
    y = ((c // 2) % 2 + delta[1]) % NY
    k = (c % 2 + delta[2]) % NK
    return x * 4 + y * 2 + k


def plus(a, b):
    return ((a[0] + b[0]) % NX, (a[1] + b[1]) % NY, (a[2] + b[2]) % NK)


def greet(targets):
    barrier = pltpu.get_barrier_semaphore()
    for target in targets:
        pl.semaphore_signal(barrier, inc=1, device_id=target, device_id_type=MESH)
    pl.semaphore_wait(barrier, len(targets))


def ctx_neighbours():
    e = lax.axis_index("exp")
    return [(ctx_at(STEP[t]), e) for t in "RLYS"]


class Gather:
    def __init__(self, number, mode, slot, send, recv):
        self.number, self.mode, self.slot = number, mode, slot
        self.send, self.recv = send, recv
        self.depth = []
        for trigger, _, _, _ in mode:
            self.depth.append(0 if trigger is None else self.depth[trigger] + 1)

    def copy(self, j, arriving):
        trigger, rel, half, to = self.mode[j]
        e = lax.axis_index("exp")
        at = plus(FROM[to], rel) if arriving else rel
        ref = self.slot(ctx_at(at), half)
        source = ref
        return pltpu.make_async_remote_copy(
            src_ref=source,
            dst_ref=ref,
            send_sem=self.send.at[self.number, j],
            recv_sem=self.recv.at[self.number, j],
            device_id=(ctx_at(STEP[to]), e),
            device_id_type=MESH,
        )

    def start(self, trigger):
        for j, transfer in enumerate(self.mode):
            if transfer[0] == trigger:
                self.copy(j, False).start()

    def arrive(self, j):
        self.copy(j, True).wait_recv()

    def events(self):
        triggers = sorted({t[0] for t in self.mode if t[0] is not None})
        out = [(0, functools.partial(self.start, None))]

        def forward(j):
            self.arrive(j)
            self.start(j)

        for j in triggers:
            out.append((self.depth[j] + 1, functools.partial(forward, j)))
        return out

    def finish(self):
        forwarded = {t[0] for t in self.mode}
        for j in range(len(self.mode)):
            if j not in forwarded:
                self.arrive(j)

    def drain(self):
        for j in range(len(self.mode)):
            self.copy(j, False).wait_send()


CHIPS = ((0, 0), (0, 1), (3, 0), (1, 0), (3, 1), (1, 1), (2, 1), (2, 0))
SOURCE = {1: 0, 3: 1, 2: 2}
ROWS = 64
PIECES = ((X_THEN_Y, 16), (Y_THEN_X, 48))


class LocalGather(Gather):
    def copy(self, j, arriving):
        trigger, rel, half, to = self.mode[j]
        e = lax.axis_index("exp")
        there = plus(FROM[to], rel)
        here = there if arriving else plus(rel, (0, 0, 0))
        return pltpu.make_async_remote_copy(
            src_ref=self.slot(here, half),
            dst_ref=self.slot(there, half),
            send_sem=self.send.at[self.number, j],
            recv_sem=self.recv.at[self.number, j],
            device_id=(ctx_at(STEP[to]), e),
            device_id_type=MESH,
        )


def expert_kernel(
    arrived, gate, up, down, residual, mix, out,
    tok, wgu, wdn, hid, part, from_sib, x_first, y_sum, y_first, x_sum, slots, returned,
    ag_send, ag_recv, w_sem, own_sem, rs_send, rs_recv, back_send, back_recv,
):
    c, e = lax.axis_index("ctx"), lax.axis_index("exp")
    peers = [lax.rem(e + d, 8) for d in range(1, 8)]
    f32, bf16 = jnp.float32, jnp.bfloat16
    units, width = down.shape[1:]
    half_width = width // 2
    own_copy = pltpu.make_async_copy(arrived, tok.at[0, pl.ds(0, ROWS), :], own_sem)
    own_copy.start()
    loads = [
        pltpu.make_async_copy(gate.at[0], wgu.at[:, pl.ds(0, units)], w_sem.at[0]),
        pltpu.make_async_copy(up.at[0], wgu.at[:, pl.ds(units, units)], w_sem.at[1]),
        pltpu.make_async_copy(down.at[0], wdn, w_sem.at[2]),
    ]
    greet(ctx_neighbours() + [(ctx_at((2, 0, 0)), e)] + [(c, to) for to in peers])
    own_copy.wait()

    pieces, first, second, begin = [], [], [], 0
    for number, (mode, rows) in enumerate(PIECES):

        def slot(rel, half, begin=begin, rows=rows):
            g, start = CHIPS.index(rel[:2]), rel[2] * ROWS + begin
            if half is None:
                return tok.at[g, pl.ds(start, rows), :]
            return tok.at[g, pl.ds(start, rows), pl.ds(half * half_width, half_width)]

        pieces.append(LocalGather(number, mode, slot, ag_send, ag_recv))
        (first if mode is Y_THEN_X else second).append(pieces[-1])
        begin += rows
    for piece in pieces:
        piece.start(None)
    for load in loads:
        load.start()

    def forward(group, *js):
        for j in js:
            for piece in group:
                piece.arrive(j)
                piece.start(j)

    def need(group, *js):
        for j in js:
            for piece in group:
                piece.arrive(j)

    def rs_copy(j, source, target, to):
        return pltpu.make_async_remote_copy(
            src_ref=source, dst_ref=target, send_sem=rs_send.at[j], recv_sem=rs_recv.at[j],
            device_id=(ctx_at(to), e), device_id_type=MESH,
        )

    mine = pl.ds(0, ROWS)
    lhs, rhs = pl.ds(0, x_first.shape[-1]), pl.ds(x_first.shape[-1], x_sum.shape[-1])

    def to_sib(g):
        return rs_copy(g, part.at[g, pl.ds(ROWS, ROWS), :], from_sib.at[g], (0, 0, 1))

    x_first_copy, y_first_copy, x_sum_copy = {}, {}, {}
    for g, (dx, dy) in enumerate(CHIPS):
        if dx:
            s = SOURCE[dx]
            x_first_copy[dx, dy] = rs_copy(8 + s * 2 + dy, part.at[g, mine, lhs], x_first.at[s, dy], (dx, 0, 0))
            if not dy:
                x_sum_copy[dx] = rs_copy(14 + s, part.at[g, mine, rhs], x_sum.at[s], (dx, 0, 0))
        if dy:
            y_first_copy[dx] = rs_copy(17 + dx, part.at[g, mine, rhs], y_first.at[dx], (0, 1, 0))
    y_sum_copy = rs_copy(21, part.at[1, mine, lhs], y_sum, (0, 1, 0))

    def merge(g):
        to_sib(g).wait_recv()
        part[g, mine, :] = (part[g, mine, :].astype(f32) + from_sib[g].astype(f32)).astype(bf16)

    def send(g):
        dx, dy = CHIPS[g]
        if dx:
            x_first_copy[dx, dy].start()
        if dy:
            y_first_copy[dx].start()

    def send_right(dx):
        g = CHIPS.index((dx, 0))
        y_first_copy[dx].wait_recv()
        part[g, mine, rhs] = (part[g, mine, rhs].astype(f32) + y_first[dx].astype(f32)).astype(bf16)
        if dx:
            x_sum_copy[dx].start()

    before = {
        0: lambda: (
            forward(second, 2), forward(first, 0), need(first, 3), need(second, 3), loads[0].wait(), loads[1].wait(),
        ),
        1: lambda: (
            need(first, 6), need(second, 10), forward(first, 1, 2),
        ),
        2: lambda: (forward(second, 4, 7), need(first, 8), need(second, 6)),
        3: lambda: (forward(first, 4, 5), need(first, 10), need(second, 9)),
        4: lambda: (forward(first, 7, 9), need(first, 12), need(second, 15)),
        5: lambda: (forward(first, 11, 13), need(first, 14), need(second, 16)),
        6: lambda: (need(first, 17, 18), need(second, 17, 18)),
        7: lambda: (need(first, 15, 16), need(second, 12, 14)),
    }
    between = {
        0: lambda: (forward(second, 0, 1), loads[2].wait()),
        3: lambda: (forward(second, 5, 8), send_right(0)),
        5: lambda: (forward(second, 11, 13),),
        6: lambda: (send_right(3),),
        7: lambda: (send_right(1),),
    }

    def at_step(g, actions):
        for at, action in actions.items():

            @pl.when(g == at)
            def _(action=action):
                action()

    def step(g, _):
        at_step(g, before)
        both = jnp.dot(tok[g], wgu[...], preferred_element_type=f32)
        v = both[:, :units]
        hid[...] = (v / (1.0 + jnp.exp(-v)) * both[:, units:]).astype(bf16)

        @pl.when(g > 0)
        def _():
            merge(g - 1)

        for at in range(1, 8):
            pl.when(g == at)(functools.partial(send, at - 1))
        at_step(g, between)
        part[g] = jnp.dot(hid[...], wdn[...], preferred_element_type=f32).astype(bf16)
        to_sib(g).start()
        return 0

    lax.fori_loop(0, 8, step, 0)
    merge(7)
    send(7)
    send_right(2)

    moves = {}

    def give_back(h, value):
        cols = rhs if h else lhs
        slots[:, :, cols] = value.reshape(8, ROWS // 8, -1).astype(bf16)
        moves[h] = [
            pltpu.make_async_remote_copy(
                src_ref=slots.at[to, :, cols],
                dst_ref=returned.at[e, :, cols],
                send_sem=back_send.at[h, d],
                recv_sem=back_recv.at[h, d],
                device_id=(c, to),
                device_id_type=MESH,
            )
            for d, to in enumerate(peers)
        ]
        for move in moves[h]:
            move.start()
        returned[e, :, cols] = slots[e, :, cols]

    for dx in (1, 3, 2):
        x_first_copy[dx, 1].wait_recv()
    total = part[1, mine, lhs].astype(f32)
    for s in range(3):
        total = total + x_first[s, 1].astype(f32)
    part[1, mine, lhs] = total.astype(bf16)
    y_sum_copy.start()
    for dx in (1, 3, 2):
        x_sum_copy[dx].wait_recv()
    total = part[0, mine, rhs].astype(f32)
    for s in range(3):
        total = total + x_sum[s].astype(f32)
    give_back(1, total)
    for dx in (1, 3, 2):
        x_first_copy[dx, 0].wait_recv()
    total = part[0, mine, lhs].astype(f32)
    for s in range(3):
        total = total + x_first[s, 0].astype(f32)
    y_sum_copy.wait_recv()
    give_back(0, total + y_sum[...].astype(f32))
    hi = mix[...].astype(bf16)
    lo = (mix[...] - hi.astype(f32)).astype(bf16)
    for h, cols in ((1, rhs), (0, lhs)):
        for move in moves[h]:
            move.wait_recv()
        outcome = returned[:, :, cols].astype(f32).reshape(ROWS, -1).astype(bf16)
        mixture = jnp.dot(hi, outcome, preferred_element_type=f32) + jnp.dot(lo, outcome, preferred_element_type=f32)
        out[:, cols] = (residual[:, cols].astype(f32) + mixture).astype(bf16)
    for h in range(2):
        for move in moves[h]:
            move.wait_send()
    for piece in pieces:
        piece.drain()
    for copies in (x_first_copy, y_first_copy, x_sum_copy):
        for copy in copies.values():
            copy.wait_send()
    y_sum_copy.wait_send()
    for g in range(8):
        to_sib(g).wait_send()


def experts(arrived, w_gate, w_up, w_down, residual, mix):
    rows, width = arrived.shape
    ff = w_gate.shape[2]
    left = width * 5 // 8
    bf16 = jnp.bfloat16
    return pl.pallas_call(
        expert_kernel,
        out_shape=jax.ShapeDtypeStruct(residual.shape, bf16),
        in_specs=[pl.BlockSpec(memory_space=pltpu.HBM)] * 4 + [pl.BlockSpec(memory_space=pltpu.VMEM)] * 2,
        out_specs=pl.BlockSpec(memory_space=pltpu.VMEM),
        scratch_shapes=[
            pltpu.VMEM((8, 2 * rows, width), bf16),
            pltpu.VMEM((width, 2 * ff), bf16),
            pltpu.VMEM((ff, width), bf16),
            pltpu.VMEM((2 * rows, ff), bf16),
            pltpu.VMEM((8, 2 * rows, width), bf16),
            pltpu.VMEM((8, rows, width), bf16),
            pltpu.VMEM((3, 2, rows, left), bf16),
            pltpu.VMEM((rows, left), bf16),
            pltpu.VMEM((4, rows, width - left), bf16),
            pltpu.VMEM((3, rows, width - left), bf16),
            pltpu.VMEM((8, rows // 8, width), bf16),
            pltpu.VMEM((8, rows // 8, width), bf16),
            pltpu.SemaphoreType.DMA((len(PIECES), N_TRANSFERS)),
            pltpu.SemaphoreType.DMA((len(PIECES), N_TRANSFERS)),
            pltpu.SemaphoreType.DMA((3,)),
            pltpu.SemaphoreType.DMA,
            pltpu.SemaphoreType.DMA((22,)),
            pltpu.SemaphoreType.DMA((22,)),
            pltpu.SemaphoreType.DMA((2, 7)),
            pltpu.SemaphoreType.DMA((2, 7)),
        ],
        compiler_params=pltpu.CompilerParams(
            collective_id=3, has_side_effects=True, vmem_limit_bytes=58 * 1024 * 1024
        ),
        name="experts",
    )(arrived, w_gate, w_up, w_down, residual, mix)


def mixer_kernel(
    hidden, attn_gain, w_query, w_key, w_value, w_out, prior_keys, prior_values, cosine, sine, ffn_gain, select,
    residual_out, arrived_out,
    normed, wkv, wq, kv, wo, query, scores, best, mass, blend, attended, part, from_exp, slots,
    send, recv, local, rs_send, rs_recv, to_send, to_recv,
):
    c, e = lax.axis_index("ctx"), lax.axis_index("exp")
    f32, bf16 = jnp.float32, jnp.bfloat16
    tokens, width = hidden.shape
    depth = w_query.shape[0]
    heads = w_query.shape[1] // HEAD_DIM
    tok_dev = residual_out.shape[0]
    out_cols = w_out.shape[1]
    span = kv.shape[0] // 2

    own_rows = pl.ds(pl.multiple_of(c * depth, depth), depth)
    own_keys = pl.ds(pl.multiple_of(c * tokens, tokens), tokens)
    left, right = pl.ds(0, HEAD_DIM), pl.ds(HEAD_DIM, HEAD_DIM)
    copies = [
        pltpu.make_async_copy(source, target, local.at[i])
        for i, (source, target) in enumerate(
            (
                (w_key, wkv.at[own_rows, left]),
                (w_value, wkv.at[own_rows, right]),
                (prior_keys, kv.at[own_keys, left]),
                (prior_values, kv.at[own_keys, right]),
                (w_query, wq.at[own_rows, :]),
                (w_out, wo.at[:, pl.ds(pl.multiple_of(c * out_cols, out_cols), out_cols)]),
            )
        )
    ]
    for copy in copies:
        copy.start()
    greet(
        [(ctx_at(step), e) for step in STEP.values()] + [(c, lax.rem(e + d, 8)) for d in range(1, 8)]
    )
    for copy in copies:
        copy.wait()

    def rows_of(buffer, stride, base, first, rows):
        def slot(index, half):
            part_rows = rows if half is None else rows // 2
            start = base + index * stride + first + (0 if half is None else half * part_rows)
            return buffer.at[pl.ds(pl.multiple_of(start, 16), part_rows), :]

        return slot

    def block_of(buffer, first, rows):
        def slot(index, half):
            part_rows = rows if half is None else rows // 2
            return buffer.at[
                pl.ds(first + (0 if half is None else half * part_rows), part_rows),
                pl.ds(pl.multiple_of(index * out_cols, out_cols), out_cols),
            ]

        return slot

    plan = []
    for buffer, stride in ((wkv, depth), (kv, tokens), (wq, depth)):
        for i, mode in enumerate((Y_THEN_X, X_THEN_Y)):
            plan.append((mode, rows_of(buffer, stride, 0, i * stride // 2, stride // 2)))
    for i, mode in enumerate((Y_THEN_X, X_THEN_Y)):
        rows = w_out.shape[0] // 2
        plan.append((mode, block_of(wo, i * rows, rows)))
    pieces = [Gather(n, mode, slot, send, recv) for n, (mode, slot) in enumerate(plan)]
    now = Gather(len(pieces), DIRECT, rows_of(kv, tokens, span, 0, tokens), send, recv)

    tile = 16

    def norm_rows(i, _):
        rows = pl.ds(pl.multiple_of(i * tile, tile), tile)
        wide = hidden[rows, :].astype(f32)
        inverse = lax.rsqrt(jnp.mean(wide * wide, axis=-1, keepdims=True) + 1e-05)
        normed[rows, :] = (wide * inverse * attn_gain[...].astype(f32)[None]).astype(bf16)
        return 0

    def normalise():
        lax.fori_loop(0, tokens // tile, norm_rows, 0)

    def turned(a):
        return (a * cosine[...] + pltpu.roll(a, HEAD_DIM // 2, 1) * sine[...]).astype(bf16)

    def keys_and_values():
        for piece in pieces[:2]:
            piece.finish()
        both = jnp.dot(normed[...], wkv[...], preferred_element_type=f32)
        rows = pl.ds(pl.multiple_of(span + c * tokens, tokens), tokens)
        kv[rows, left] = turned(both[:, :HEAD_DIM])
        kv[rows, right] = both[:, HEAD_DIM:].astype(bf16)
        now.start(None)

    def queries():
        for piece in pieces[4:6]:
            piece.finish()
        raw = jnp.dot(normed[...], wq[...], preferred_element_type=f32)
        for g in range(heads):
            query[pl.ds(g * tokens, tokens), :] = turned(raw[:, g * HEAD_DIM:(g + 1) * HEAD_DIM])

    count = heads * tokens
    block = 2 * tokens
    blocks = span // block
    inverse_root = 1.0 / math.sqrt(HEAD_DIM)

    def score(start, size):
        keys = kv[pl.ds(pl.multiple_of(start, tokens), size), left]
        return lax.dot_general(query[...], keys, (((1,), (1,)), ((), ())), preferred_element_type=f32) * inverse_root

    def masks():
        row = lax.broadcasted_iota(jnp.int32, (count, tokens), 0) % tokens
        col = lax.broadcasted_iota(jnp.int32, (count, tokens), 1)
        return row, col

    def all_scores():
        for piece in pieces[2:4] + [now]:
            piece.finish()
        row, col = masks()
        first = score(c * tokens, block)
        head_part = jnp.where(col > row, first[:, :tokens], -1e30)
        scores[:, pl.ds(0, tokens)] = head_part
        scores[:, pl.ds(tokens, tokens)] = first[:, tokens:]
        last = jnp.where(col <= row, score(c * tokens + span, tokens), -1e30)
        scores[:, pl.ds(span, tokens)] = last
        best[...] = jnp.maximum(jnp.maximum(head_part, first[:, tokens:]), last)

        def body(b, _):
            s = score(c * tokens + b * block, block)
            scores[:, pl.ds(pl.multiple_of(b * block, block), block)] = s
            best[...] = jnp.maximum(best[...], jnp.maximum(s[:, :tokens], s[:, tokens:]))
            return 0

        lax.fori_loop(1, blocks, body, 0)
        best[...] = jnp.broadcast_to(jnp.max(best[...], axis=1, keepdims=True), best.shape)

    def blended():
        top = best[:, pl.ds(0, 1)]
        p = jnp.exp(scores[:, pl.ds(span, tokens)] - top)
        mass[...] = p
        values = kv[pl.ds(pl.multiple_of(c * tokens + span, tokens), tokens), right]
        blend[...] = jnp.dot(p.astype(bf16), values, preferred_element_type=f32)

        def body(b, _):
            p = jnp.exp(scores[:, pl.ds(pl.multiple_of(b * block, block), block)] - top)
            mass[...] += p[:, :tokens] + p[:, tokens:]
            values = kv[pl.ds(pl.multiple_of(c * tokens + b * block, tokens), block), right]
            blend[...] += jnp.dot(p.astype(bf16), values, preferred_element_type=f32)
            return 0

        lax.fori_loop(0, blocks, body, 0)
        result = (blend[...] / jnp.sum(mass[...], axis=1, keepdims=True)).astype(bf16)
        for g in range(heads):
            attended[:, pl.ds(g * HEAD_DIM, HEAD_DIM)] = result[g * tokens:(g + 1) * tokens, :]

    def forward_now():
        for j in range(7):
            now.arrive(j)
            now.start(j)

    timeline = []
    for piece in pieces:
        for order, (level, action) in enumerate(piece.events()):
            timeline.append((piece.number + 1.0 * level, order, action))
    timeline += [
        (1.5, 0, normalise),
        (4.5, 0, keys_and_values),
        (7.5, 0, forward_now),
        (8.05, 0, queries),
        (8.1, 0, all_scores),
        (8.6, 0, blended),
    ]
    peers = [lax.rem(e + d, 8) for d in range(1, 8)]
    plane = 4 * out_cols
    shares = {}

    def project(dx, wants):
        for piece, js in zip(pieces[6:], wants):
            for j in js:
                piece.arrive(j)
        x = lax.rem(c // 4 + dx, NX)

        cols = pl.ds(pl.multiple_of(x * plane, plane), plane)
        part[:, cols] = jnp.dot(attended[...], wo[:, cols], preferred_element_type=f32).astype(bf16)
        shares[dx] = [
            pltpu.make_async_remote_copy(
                src_ref=part.at[pl.ds(pl.multiple_of(to * tok_dev, tok_dev), tok_dev), cols],
                dst_ref=from_exp.at[d, :, cols],
                send_sem=rs_send.at[dx, d],
                recv_sem=rs_recv.at[dx, d],
                device_id=(c, to),
                device_id_type=MESH,
            )
            for d, to in enumerate(peers)
        ]
        for share in shares[dx]:
            share.start()

    timeline += [
        (9.1, 0, lambda: project(0, ((3, 6), (3, 10)))),
        (9.2, 0, lambda: project(3, ((8, 12), (6, 15)))),
        (9.3, 0, lambda: project(1, ((10, 14), (9, 16)))),
        (11.0, 0, lambda: project(2, ((15, 16, 17, 18), (12, 14, 17, 18)))),
    ]
    for _, _, action in sorted(timeline, key=lambda item: item[:2]):
        action()
    for dx in (0, 3, 1, 2):
        for share in shares[dx]:
            share.wait_recv()
    mine = pl.ds(pl.multiple_of(e * tok_dev, tok_dev), tok_dev)
    total = part[mine, :].astype(f32)
    for d in range(7):
        total = total + from_exp[d].astype(f32)
    residual = (hidden[mine, :].astype(f32) + total).astype(bf16)
    residual_out[...] = residual
    wide = residual.astype(f32)
    inverse = lax.rsqrt(jnp.mean(wide * wide, axis=-1, keepdims=True) + 1e-05)
    ready = (wide * inverse * ffn_gain[...].astype(f32)[None]).astype(bf16)
    chosen = jnp.dot(select[...], ready, preferred_element_type=f32)
    slots[...] = chosen.reshape(slots.shape).astype(bf16)
    moves = [
        pltpu.make_async_remote_copy(
            src_ref=slots.at[to],
            dst_ref=arrived_out.at[e],
            send_sem=to_send.at[d],
            recv_sem=to_recv.at[d],
            device_id=(c, to),
            device_id_type=MESH,
        )
        for d, to in enumerate(peers)
    ]
    for move in moves:
        move.start()
    arrived_out[e] = slots[e]
    for piece in pieces + [now]:
        piece.drain()
    for dx in (0, 3, 1, 2):
        for share in shares[dx]:
            share.wait_send()
    for move in moves:
        move.wait_send()
    for move in moves:
        move.wait_recv()


def mixer(hidden, attn_gain, w_query, w_key, w_value, w_out, prior_keys, prior_values, cosine, sine, ffn_gain, select):
    tokens, width = hidden.shape
    depth, q_cols = w_query.shape
    bf16, f32 = jnp.bfloat16, jnp.float32
    span = 16 * tokens
    count = q_cols // HEAD_DIM * tokens
    vmem = pl.BlockSpec(memory_space=pltpu.VMEM)
    anywhere = pl.BlockSpec(memory_space=pltpu.HBM)
    return pl.pallas_call(
        mixer_kernel,
        out_shape=[
            jax.ShapeDtypeStruct((tokens // 8, width), bf16),
            jax.ShapeDtypeStruct((8, select.shape[0] // 8, width), bf16),
        ],
        in_specs=[vmem, vmem] + [anywhere] * 6 + [vmem] * 4,
        out_specs=[vmem] * 2,
        scratch_shapes=[
            pltpu.VMEM((tokens, width), bf16),
            pltpu.VMEM((16 * depth, 2 * HEAD_DIM), bf16),
            pltpu.VMEM((16 * depth, q_cols), bf16),
            pltpu.VMEM((2 * span, 2 * HEAD_DIM), bf16),
            pltpu.VMEM((w_out.shape[0], width), bf16),
            pltpu.VMEM((count, HEAD_DIM), bf16),
            pltpu.VMEM((count, span + tokens), f32),
            pltpu.VMEM((count, tokens), f32),
            pltpu.VMEM((count, tokens), f32),
            pltpu.VMEM((count, HEAD_DIM), f32),
            pltpu.VMEM((tokens, q_cols), bf16),
            pltpu.VMEM((tokens, width), bf16),
            pltpu.VMEM((7, tokens // 8, width), bf16),
            pltpu.VMEM((8, select.shape[0] // 8, width), bf16),
            pltpu.SemaphoreType.DMA((9, N_TRANSFERS)),
            pltpu.SemaphoreType.DMA((9, N_TRANSFERS)),
            pltpu.SemaphoreType.DMA((6,)),
            pltpu.SemaphoreType.DMA((4, 7)),
            pltpu.SemaphoreType.DMA((4, 7)),
            pltpu.SemaphoreType.DMA((7,)),
            pltpu.SemaphoreType.DMA((7,)),
        ],
        compiler_params=pltpu.CompilerParams(
            collective_id=0, has_side_effects=True, vmem_limit_bytes=60 * 1024 * 1024
        ),
        name="mixer",
    )(hidden, attn_gain, w_query, w_key, w_value, w_out, prior_keys, prior_values, cosine, sine, ffn_gain, select)


def local(
    hidden_in,
    attn_gain,
    w_query,
    w_key,
    w_value,
    w_out,
    prior_keys,
    prior_values,
    stretch_offset,
    ffn_gain,
    w_gate,
    w_up,
    w_down,
    expert_ids,
    gate_weights,
):
    exp_count = lax.axis_size("exp")
    ctx_index = lax.axis_index("ctx")
    exp_index = lax.axis_index("exp")
    local_len, model_width = hidden_in.shape
    tok_dev = local_len // exp_count
    positions = stretch_offset[0] + ctx_index * local_len + jnp.arange(local_len, dtype=jnp.int32)
    half_dim = HEAD_DIM // 2
    frequency = jnp.exp(jnp.arange(half_dim).astype(jnp.float32) * (-2.0 * math.log(1000000.0) / HEAD_DIM))
    angles = positions.astype(jnp.float32)[:, None] * frequency[None, :]
    cosine, sine = jnp.cos(angles), jnp.sin(angles)
    capacity = 4 * tok_dev // exp_count
    device_row = (ctx_index * exp_count + exp_index) * tok_dev
    my_ids = lax.dynamic_slice_in_dim(expert_ids, device_row, tok_dev, 0)
    flat = my_ids.reshape(-1)
    same = flat[:, None] == flat[None, :]
    earlier = jnp.arange(2 * tok_dev)[:, None] < jnp.arange(2 * tok_dev)[None, :]
    place = flat * capacity + jnp.sum(same & earlier, axis=0, dtype=jnp.int32)
    place = place.reshape(tok_dev, 2)
    slot = jnp.arange(exp_count * capacity, dtype=jnp.int32)
    select = ((slot[:, None] == place[None, :, 0]) | (slot[:, None] == place[None, :, 1])).astype(jnp.bfloat16)
    mix = jnp.where(place[:, :1] == slot[None, :], gate_weights[:, :1], 0.0) + jnp.where(
        place[:, 1:] == slot[None, :], gate_weights[:, 1:], 0.0
    )
    residual, arrived = mixer(
        hidden_in,
        attn_gain,
        w_query,
        w_key,
        w_value,
        w_out,
        prior_keys,
        prior_values,
        jnp.concatenate([cosine, cosine], axis=1),
        jnp.concatenate([-sine, sine], axis=1),
        ffn_gain,
        select,
    )
    return experts(arrived.reshape(-1, model_width), w_gate, w_up, w_down, residual, mix)


def solution(mesh):
    in_specs = (
        P("ctx", None),
        P(),
        P("ctx", "exp"),
        P("ctx", "exp"),
        P("ctx", "exp"),
        P("exp", "ctx"),
        P("ctx", "exp"),
        P("ctx", "exp"),
        P(),
        P(),
        P("exp", None, "ctx"),
        P("exp", None, "ctx"),
        P("exp", "ctx", None),
        P(),
        P(("ctx", "exp"), None),
    )
    out_specs = P(("ctx", "exp"), None)
    return jax.shard_map(local, mesh=mesh, in_specs=in_specs, out_specs=out_specs, check_vma=False)
```

```python
import functools
import math

import jax
import jax.numpy as jnp
from jax import lax
from jax.experimental import pallas as pl
from jax.experimental.pallas import tpu as pltpu
from jax.sharding import PartitionSpec as P

HEADS = 32
KV_HEADS = 8
HEAD_DIM = 128
MESH = pl.DeviceIdType.MESH
NX, NY, NK = 4, 2, 2

Y_THEN_X = (
    (None, (0, 0, 0), None, "Y"),
    (None, (0, 0, 0), None, "R"),
    (None, (0, 0, 0), None, "L"),
    (None, (0, 0, 0), None, "S"),
    (0, (0, 1, 0), None, "R"),
    (0, (0, 1, 0), None, "L"),
    (0, (0, 1, 0), None, "S"),
    (1, (-1, 0, 0), 0, "R"),
    (1, (-1, 0, 0), None, "S"),
    (2, (1, 0, 0), 1, "L"),
    (2, (1, 0, 0), None, "S"),
    (4, (-1, 1, 0), 0, "R"),
    (4, (-1, 1, 0), None, "S"),
    (5, (1, 1, 0), 1, "L"),
    (5, (1, 1, 0), None, "S"),
    (7, (2, 0, 0), 0, "S"),
    (9, (2, 0, 0), 1, "S"),
    (11, (2, 1, 0), 0, "S"),
    (13, (2, 1, 0), 1, "S"),
)
X_THEN_Y = (
    (None, (0, 0, 0), None, "R"),
    (None, (0, 0, 0), None, "L"),
    (None, (0, 0, 0), None, "Y"),
    (None, (0, 0, 0), None, "S"),
    (0, (-1, 0, 0), 0, "R"),
    (0, (-1, 0, 0), None, "Y"),
    (0, (-1, 0, 0), None, "S"),
    (1, (1, 0, 0), 1, "L"),
    (1, (1, 0, 0), None, "Y"),
    (1, (1, 0, 0), None, "S"),
    (2, (0, 1, 0), None, "S"),
    (4, (2, 0, 0), 0, "Y"),
    (4, (2, 0, 0), 0, "S"),
    (7, (2, 0, 0), 1, "Y"),
    (7, (2, 0, 0), 1, "S"),
    (5, (-1, 1, 0), None, "S"),
    (8, (1, 1, 0), None, "S"),
    (11, (2, 1, 0), 0, "S"),
    (13, (2, 1, 0), 1, "S"),
)
DIRECT = tuple((None, (0, 0, 0), None, to) for to in ("R", "L", "Y", "O", "RY", "LY", "OY", "S")) + (
    (0, (-1, 0, 0), None, "S"),
    (1, (1, 0, 0), None, "S"),
    (2, (0, 1, 0), None, "S"),
    (3, (2, 0, 0), None, "S"),
    (4, (-1, 1, 0), None, "S"),
    (5, (1, 1, 0), None, "S"),
    (6, (2, 1, 0), None, "S"),
)
N_TRANSFERS = 19
STEP = {
    "R": (1, 0, 0), "L": (-1, 0, 0), "Y": (0, 1, 0), "S": (0, 0, 1),
    "O": (2, 0, 0), "RY": (1, 1, 0), "LY": (-1, 1, 0), "OY": (2, 1, 0),
}
FROM = {to: (-step[0], step[1], step[2]) for to, step in STEP.items()}


def ctx_at(delta):
    c = lax.axis_index("ctx")
    x = (c // 4 + delta[0] + NX) % NX
    y = ((c // 2) % 2 + delta[1]) % NY
    k = (c % 2 + delta[2]) % NK
    return x * 4 + y * 2 + k


def plus(a, b):
    return ((a[0] + b[0]) % NX, (a[1] + b[1]) % NY, (a[2] + b[2]) % NK)


def greet(targets):
    barrier = pltpu.get_barrier_semaphore()
    for target in targets:
        pl.semaphore_signal(barrier, inc=1, device_id=target, device_id_type=MESH)
    pl.semaphore_wait(barrier, len(targets))


def ctx_neighbours():
    e = lax.axis_index("exp")
    return [(ctx_at(STEP[t]), e) for t in "RLYS"]


class Gather:
    def __init__(self, number, mode, slot, send, recv):
        self.number, self.mode, self.slot = number, mode, slot
        self.send, self.recv = send, recv
        self.depth = []
        for trigger, _, _, _ in mode:
            self.depth.append(0 if trigger is None else self.depth[trigger] + 1)

    def copy(self, j, arriving):
        trigger, rel, half, to = self.mode[j]
        e = lax.axis_index("exp")
        at = plus(FROM[to], rel) if arriving else rel
        ref = self.slot(ctx_at(at), half)
        source = ref
        return pltpu.make_async_remote_copy(
            src_ref=source,
            dst_ref=ref,
            send_sem=self.send.at[self.number, j],
            recv_sem=self.recv.at[self.number, j],
            device_id=(ctx_at(STEP[to]), e),
            device_id_type=MESH,
        )

    def start(self, trigger):
        for j, transfer in enumerate(self.mode):
            if transfer[0] == trigger:
                self.copy(j, False).start()

    def arrive(self, j):
        self.copy(j, True).wait_recv()

    def events(self):
        triggers = sorted({t[0] for t in self.mode if t[0] is not None})
        out = [(0, functools.partial(self.start, None))]

        def forward(j):
            self.arrive(j)
            self.start(j)

        for j in triggers:
            out.append((self.depth[j] + 1, functools.partial(forward, j)))
        return out

    def finish(self):
        forwarded = {t[0] for t in self.mode}
        for j in range(len(self.mode)):
            if j not in forwarded:
                self.arrive(j)

    def drain(self):
        for j in range(len(self.mode)):
            self.copy(j, False).wait_send()


CHIPS = ((0, 0), (0, 1), (3, 0), (1, 0), (3, 1), (1, 1), (2, 1), (2, 0))
SOURCE = {1: 0, 3: 1, 2: 2}
ROWS = 64
PIECES = ((Y_THEN_X, 48), (X_THEN_Y, 16))


class LocalGather(Gather):
    def copy(self, j, arriving):
        trigger, rel, half, to = self.mode[j]
        e = lax.axis_index("exp")
        there = plus(FROM[to], rel)
        here = there if arriving else plus(rel, (0, 0, 0))
        return pltpu.make_async_remote_copy(
            src_ref=self.slot(here, half),
            dst_ref=self.slot(there, half),
            send_sem=self.send.at[self.number, j],
            recv_sem=self.recv.at[self.number, j],
            device_id=(ctx_at(STEP[to]), e),
            device_id_type=MESH,
        )


def expert_kernel(
    arrived, gate, up, down, residual, mix, out,
    tok, wgu, wdn, hid, part, from_sib, x_first, y_sum, y_first, x_sum, slots, returned,
    ag_send, ag_recv, w_sem, own_sem, rs_send, rs_recv, back_send, back_recv,
):
    c, e = lax.axis_index("ctx"), lax.axis_index("exp")
    peers = [lax.rem(e + d, 8) for d in range(1, 8)]
    f32, bf16 = jnp.float32, jnp.bfloat16
    units, width = down.shape[1:]
    half_width = width // 2
    own_copy = pltpu.make_async_copy(arrived, tok.at[0, pl.ds(0, ROWS), :], own_sem)
    own_copy.start()
    loads = [
        pltpu.make_async_copy(gate.at[0], wgu.at[:, pl.ds(0, units)], w_sem.at[0]),
        pltpu.make_async_copy(up.at[0], wgu.at[:, pl.ds(units, units)], w_sem.at[1]),
        pltpu.make_async_copy(down.at[0], wdn, w_sem.at[2]),
    ]
    greet(ctx_neighbours() + [(ctx_at((2, 0, 0)), e)] + [(c, to) for to in peers])
    own_copy.wait()

    pieces, first, second, begin = [], [], [], 0
    for number, (mode, rows) in enumerate(PIECES):

        def slot(rel, half, begin=begin, rows=rows):
            g, start = CHIPS.index(rel[:2]), rel[2] * ROWS + begin
            if half is None:
                return tok.at[g, pl.ds(start, rows), :]
            return tok.at[g, pl.ds(start, rows), pl.ds(half * half_width, half_width)]

        pieces.append(LocalGather(number, mode, slot, ag_send, ag_recv))
        (first if mode is Y_THEN_X else second).append(pieces[-1])
        begin += rows
    for piece in pieces:
        piece.start(None)
    for load in loads:
        load.start()

    def forward(group, *js):
        for j in js:
            for piece in group:
                piece.arrive(j)
                piece.start(j)

    def need(group, *js):
        for j in js:
            for piece in group:
                piece.arrive(j)

    def rs_copy(j, source, target, to):
        return pltpu.make_async_remote_copy(
            src_ref=source, dst_ref=target, send_sem=rs_send.at[j], recv_sem=rs_recv.at[j],
            device_id=(ctx_at(to), e), device_id_type=MESH,
        )

    mine = pl.ds(0, ROWS)
    lhs, rhs = pl.ds(0, x_first.shape[-1]), pl.ds(x_first.shape[-1], x_sum.shape[-1])

    def to_sib(g):
        return rs_copy(g, part.at[g, pl.ds(ROWS, ROWS), :], from_sib.at[g], (0, 0, 1))

    x_first_copy, y_first_copy, x_sum_copy = {}, {}, {}
    for g, (dx, dy) in enumerate(CHIPS):
        if dx:
            s = SOURCE[dx]
            x_first_copy[dx, dy] = rs_copy(8 + s * 2 + dy, part.at[g, mine, lhs], x_first.at[s, dy], (dx, 0, 0))
            if not dy:
                x_sum_copy[dx] = rs_copy(14 + s, part.at[g, mine, rhs], x_sum.at[s], (dx, 0, 0))
        if dy:
            y_first_copy[dx] = rs_copy(17 + dx, part.at[g, mine, rhs], y_first.at[dx], (0, 1, 0))
    y_sum_copy = rs_copy(21, part.at[1, mine, lhs], y_sum, (0, 1, 0))

    def merge(g):
        to_sib(g).wait_recv()
        part[g, mine, :] = (part[g, mine, :].astype(f32) + from_sib[g].astype(f32)).astype(bf16)

    def send(g):
        dx, dy = CHIPS[g]
        if dx:
            x_first_copy[dx, dy].start()
        if dy:
            y_first_copy[dx].start()

    def send_right(dx):
        g = CHIPS.index((dx, 0))
        y_first_copy[dx].wait_recv()
        part[g, mine, rhs] = (part[g, mine, rhs].astype(f32) + y_first[dx].astype(f32)).astype(bf16)
        if dx:
            x_sum_copy[dx].start()

    before = {
        0: lambda: (
            forward(second, 2), forward(first, 0), need(first, 3), need(second, 3), loads[0].wait(), loads[1].wait(),
        ),
        1: lambda: (
            need(first, 6), need(second, 10), forward(first, 1, 2),
        ),
        2: lambda: (forward(second, 4, 7), need(first, 8), need(second, 6)),
        3: lambda: (forward(first, 4, 5), need(first, 10), need(second, 9)),
        4: lambda: (forward(first, 7, 9), need(first, 12), need(second, 15)),
        5: lambda: (forward(first, 11, 13), need(first, 14), need(second, 16)),
        6: lambda: (need(first, 17, 18), need(second, 17, 18)),
        7: lambda: (need(first, 15, 16), need(second, 12, 14)),
    }
    between = {
        0: lambda: (forward(second, 0, 1), loads[2].wait()),
        3: lambda: (forward(second, 5, 8), send_right(0)),
        5: lambda: (forward(second, 11, 13),),
        6: lambda: (send_right(3),),
        7: lambda: (send_right(1),),
    }

    def at_step(g, actions):
        for at, action in actions.items():

            @pl.when(g == at)
            def _(action=action):
                action()

    def step(g, _):
        at_step(g, before)
        both = jnp.dot(tok[g], wgu[...], preferred_element_type=f32)
        v = both[:, :units]
        hid[...] = (v / (1.0 + jnp.exp(-v)) * both[:, units:]).astype(bf16)

        @pl.when(g > 0)
        def _():
            merge(g - 1)

        for at in range(1, 8):
            pl.when(g == at)(functools.partial(send, at - 1))
        at_step(g, between)
        part[g] = jnp.dot(hid[...], wdn[...], preferred_element_type=f32).astype(bf16)
        to_sib(g).start()
        return 0

    lax.fori_loop(0, 8, step, 0)
    merge(7)
    send(7)
    send_right(2)

    moves = {}

    def give_back(h, value):
        cols = rhs if h else lhs
        slots[:, :, cols] = value.reshape(8, ROWS // 8, -1).astype(bf16)
        moves[h] = [
            pltpu.make_async_remote_copy(
                src_ref=slots.at[to, :, cols],
                dst_ref=returned.at[e, :, cols],
                send_sem=back_send.at[h, d],
                recv_sem=back_recv.at[h, d],
                device_id=(c, to),
                device_id_type=MESH,
            )
            for d, to in enumerate(peers)
        ]
        for move in moves[h]:
            move.start()
        returned[e, :, cols] = slots[e, :, cols]

    for dx in (1, 3, 2):
        x_first_copy[dx, 1].wait_recv()
    total = part[1, mine, lhs].astype(f32)
    for s in range(3):
        total = total + x_first[s, 1].astype(f32)
    part[1, mine, lhs] = total.astype(bf16)
    y_sum_copy.start()
    for dx in (1, 3, 2):
        x_sum_copy[dx].wait_recv()
    total = part[0, mine, rhs].astype(f32)
    for s in range(3):
        total = total + x_sum[s].astype(f32)
    give_back(1, total)
    for dx in (1, 3, 2):
        x_first_copy[dx, 0].wait_recv()
    total = part[0, mine, lhs].astype(f32)
    for s in range(3):
        total = total + x_first[s, 0].astype(f32)
    y_sum_copy.wait_recv()
    give_back(0, total + y_sum[...].astype(f32))
    hi = mix[...].astype(bf16)
    lo = (mix[...] - hi.astype(f32)).astype(bf16)
    for h, cols in ((1, rhs), (0, lhs)):
        for move in moves[h]:
            move.wait_recv()
        outcome = returned[:, :, cols].astype(f32).reshape(ROWS, -1).astype(bf16)
        mixture = jnp.dot(hi, outcome, preferred_element_type=f32) + jnp.dot(lo, outcome, preferred_element_type=f32)
        out[:, cols] = (residual[:, cols].astype(f32) + mixture).astype(bf16)
    for h in range(2):
        for move in moves[h]:
            move.wait_send()
    for piece in pieces:
        piece.drain()
    for copies in (x_first_copy, y_first_copy, x_sum_copy):
        for copy in copies.values():
            copy.wait_send()
    y_sum_copy.wait_send()
    for g in range(8):
        to_sib(g).wait_send()


def experts(arrived, w_gate, w_up, w_down, residual, mix):
    rows, width = arrived.shape
    ff = w_gate.shape[2]
    left = width * 5 // 8
    bf16 = jnp.bfloat16
    return pl.pallas_call(
        expert_kernel,
        out_shape=jax.ShapeDtypeStruct(residual.shape, bf16),
        in_specs=[pl.BlockSpec(memory_space=pltpu.HBM)] * 4 + [pl.BlockSpec(memory_space=pltpu.VMEM)] * 2,
        out_specs=pl.BlockSpec(memory_space=pltpu.VMEM),
        scratch_shapes=[
            pltpu.VMEM((8, 2 * rows, width), bf16),
            pltpu.VMEM((width, 2 * ff), bf16),
            pltpu.VMEM((ff, width), bf16),
            pltpu.VMEM((2 * rows, ff), bf16),
            pltpu.VMEM((8, 2 * rows, width), bf16),
            pltpu.VMEM((8, rows, width), bf16),
            pltpu.VMEM((3, 2, rows, left), bf16),
            pltpu.VMEM((rows, left), bf16),
            pltpu.VMEM((4, rows, width - left), bf16),
            pltpu.VMEM((3, rows, width - left), bf16),
            pltpu.VMEM((8, rows // 8, width), bf16),
            pltpu.VMEM((8, rows // 8, width), bf16),
            pltpu.SemaphoreType.DMA((len(PIECES), N_TRANSFERS)),
            pltpu.SemaphoreType.DMA((len(PIECES), N_TRANSFERS)),
            pltpu.SemaphoreType.DMA((3,)),
            pltpu.SemaphoreType.DMA,
            pltpu.SemaphoreType.DMA((22,)),
            pltpu.SemaphoreType.DMA((22,)),
            pltpu.SemaphoreType.DMA((2, 7)),
            pltpu.SemaphoreType.DMA((2, 7)),
        ],
        compiler_params=pltpu.CompilerParams(
            collective_id=3, has_side_effects=True, vmem_limit_bytes=58 * 1024 * 1024
        ),
        name="experts",
    )(arrived, w_gate, w_up, w_down, residual, mix)


def mixer_kernel(
    hidden, attn_gain, w_query, w_key, w_value, w_out, prior_keys, prior_values, cosine, sine, ffn_gain, select,
    residual_out, arrived_out,
    normed, wkv, wq, kv, wo, query, scores, best, mass, blend, attended, part, from_exp, slots,
    send, recv, local, rs_send, rs_recv, to_send, to_recv,
):
    c, e = lax.axis_index("ctx"), lax.axis_index("exp")
    f32, bf16 = jnp.float32, jnp.bfloat16
    tokens, width = hidden.shape
    depth = w_query.shape[0]
    heads = w_query.shape[1] // HEAD_DIM
    tok_dev = residual_out.shape[0]
    out_cols = w_out.shape[1]
    span = kv.shape[0] // 2

    own_rows = pl.ds(pl.multiple_of(c * depth, depth), depth)
    own_keys = pl.ds(pl.multiple_of(c * tokens, tokens), tokens)
    left, right = pl.ds(0, HEAD_DIM), pl.ds(HEAD_DIM, HEAD_DIM)
    copies = [
        pltpu.make_async_copy(source, target, local.at[i])
        for i, (source, target) in enumerate(
            (
                (w_key, wkv.at[own_rows, left]),
                (w_value, wkv.at[own_rows, right]),
                (prior_keys, kv.at[own_keys, left]),
                (prior_values, kv.at[own_keys, right]),
                (w_query, wq.at[own_rows, :]),
                (w_out, wo.at[:, pl.ds(pl.multiple_of(c * out_cols, out_cols), out_cols)]),
            )
        )
    ]
    for copy in copies:
        copy.start()
    greet(
        [(ctx_at(step), e) for step in STEP.values()] + [(c, lax.rem(e + d, 8)) for d in range(1, 8)]
    )
    for copy in copies:
        copy.wait()

    def rows_of(buffer, stride, base, first, rows):
        def slot(index, half):
            part_rows = rows if half is None else rows // 2
            start = base + index * stride + first + (0 if half is None else half * part_rows)
            return buffer.at[pl.ds(pl.multiple_of(start, 16), part_rows), :]

        return slot

    def block_of(buffer, first, rows):
        def slot(index, half):
            part_rows = rows if half is None else rows // 2
            return buffer.at[
                pl.ds(first + (0 if half is None else half * part_rows), part_rows),
                pl.ds(pl.multiple_of(index * out_cols, out_cols), out_cols),
            ]

        return slot

    plan = []
    for buffer, stride in ((wkv, depth), (kv, tokens), (wq, depth)):
        for i, mode in enumerate((Y_THEN_X, X_THEN_Y)):
            plan.append((mode, rows_of(buffer, stride, 0, i * stride // 2, stride // 2)))
    for i, mode in enumerate((Y_THEN_X, X_THEN_Y)):
        rows = w_out.shape[0] // 2
        plan.append((mode, block_of(wo, i * rows, rows)))
    pieces = [Gather(n, mode, slot, send, recv) for n, (mode, slot) in enumerate(plan)]
    now = Gather(len(pieces), DIRECT, rows_of(kv, tokens, span, 0, tokens), send, recv)

    tile = 16

    def norm_rows(i, _):
        rows = pl.ds(pl.multiple_of(i * tile, tile), tile)
        wide = hidden[rows, :].astype(f32)
        inverse = lax.rsqrt(jnp.mean(wide * wide, axis=-1, keepdims=True) + 1e-05)
        normed[rows, :] = (wide * inverse * attn_gain[...].astype(f32)[None]).astype(bf16)
        return 0

    def normalise():
        lax.fori_loop(0, tokens // tile, norm_rows, 0)

    def turned(a):
        return (a * cosine[...] + pltpu.roll(a, HEAD_DIM // 2, 1) * sine[...]).astype(bf16)

    def keys_and_values():
        for piece in pieces[:2]:
            piece.finish()
        both = jnp.dot(normed[...], wkv[...], preferred_element_type=f32)
        rows = pl.ds(pl.multiple_of(span + c * tokens, tokens), tokens)
        kv[rows, left] = turned(both[:, :HEAD_DIM])
        kv[rows, right] = both[:, HEAD_DIM:].astype(bf16)
        now.start(None)

    def queries():
        for piece in pieces[4:6]:
            piece.finish()
        raw = jnp.dot(normed[...], wq[...], preferred_element_type=f32)
        for g in range(heads):
            query[pl.ds(g * tokens, tokens), :] = turned(raw[:, g * HEAD_DIM:(g + 1) * HEAD_DIM])

    count = heads * tokens
    block = 2 * tokens
    blocks = span // block
    inverse_root = 1.0 / math.sqrt(HEAD_DIM)

    def score(start, size):
        keys = kv[pl.ds(pl.multiple_of(start, tokens), size), left]
        return lax.dot_general(query[...], keys, (((1,), (1,)), ((), ())), preferred_element_type=f32) * inverse_root

    def masks():
        row = lax.broadcasted_iota(jnp.int32, (count, tokens), 0) % tokens
        col = lax.broadcasted_iota(jnp.int32, (count, tokens), 1)
        return row, col

    def all_scores():
        for piece in pieces[2:4] + [now]:
            piece.finish()
        row, col = masks()
        first = score(c * tokens, block)
        head_part = jnp.where(col > row, first[:, :tokens], -1e30)
        scores[:, pl.ds(0, tokens)] = head_part
        scores[:, pl.ds(tokens, tokens)] = first[:, tokens:]
        last = jnp.where(col <= row, score(c * tokens + span, tokens), -1e30)
        scores[:, pl.ds(span, tokens)] = last
        best[...] = jnp.maximum(jnp.maximum(head_part, first[:, tokens:]), last)

        def body(b, _):
            s = score(c * tokens + b * block, block)
            scores[:, pl.ds(pl.multiple_of(b * block, block), block)] = s
            best[...] = jnp.maximum(best[...], jnp.maximum(s[:, :tokens], s[:, tokens:]))
            return 0

        lax.fori_loop(1, blocks, body, 0)
        best[...] = jnp.broadcast_to(jnp.max(best[...], axis=1, keepdims=True), best.shape)

    def blended():
        top = best[:, pl.ds(0, 1)]
        p = jnp.exp(scores[:, pl.ds(span, tokens)] - top)
        mass[...] = p
        values = kv[pl.ds(pl.multiple_of(c * tokens + span, tokens), tokens), right]
        blend[...] = jnp.dot(p.astype(bf16), values, preferred_element_type=f32)

        def body(b, _):
            p = jnp.exp(scores[:, pl.ds(pl.multiple_of(b * block, block), block)] - top)
            mass[...] += p[:, :tokens] + p[:, tokens:]
            values = kv[pl.ds(pl.multiple_of(c * tokens + b * block, tokens), block), right]
            blend[...] += jnp.dot(p.astype(bf16), values, preferred_element_type=f32)
            return 0

        lax.fori_loop(0, blocks, body, 0)
        result = (blend[...] / jnp.sum(mass[...], axis=1, keepdims=True)).astype(bf16)
        for g in range(heads):
            attended[:, pl.ds(g * HEAD_DIM, HEAD_DIM)] = result[g * tokens:(g + 1) * tokens, :]

    def forward_now():
        for j in range(7):
            now.arrive(j)
            now.start(j)

    timeline = []
    for piece in pieces:
        for order, (level, action) in enumerate(piece.events()):
            timeline.append((piece.number + 1.0 * level, order, action))
    timeline += [
        (1.5, 0, normalise),
        (4.5, 0, keys_and_values),
        (7.5, 0, forward_now),
        (8.05, 0, queries),
        (8.1, 0, all_scores),
        (8.6, 0, blended),
    ]
    peers = [lax.rem(e + d, 8) for d in range(1, 8)]
    plane = 4 * out_cols
    shares = {}

    def project(dx, wants):
        for piece, js in zip(pieces[6:], wants):
            for j in js:
                piece.arrive(j)
        x = lax.rem(c // 4 + dx, NX)

        cols = pl.ds(pl.multiple_of(x * plane, plane), plane)
        part[:, cols] = jnp.dot(attended[...], wo[:, cols], preferred_element_type=f32).astype(bf16)
        shares[dx] = [
            pltpu.make_async_remote_copy(
                src_ref=part.at[pl.ds(pl.multiple_of(to * tok_dev, tok_dev), tok_dev), cols],
                dst_ref=from_exp.at[d, :, cols],
                send_sem=rs_send.at[dx, d],
                recv_sem=rs_recv.at[dx, d],
                device_id=(c, to),
                device_id_type=MESH,
            )
            for d, to in enumerate(peers)
        ]
        for share in shares[dx]:
            share.start()

    timeline += [
        (9.1, 0, lambda: project(0, ((3, 6), (3, 10)))),
        (9.2, 0, lambda: project(3, ((8, 12), (6, 15)))),
        (9.3, 0, lambda: project(1, ((10, 14), (9, 16)))),
        (11.0, 0, lambda: project(2, ((15, 16, 17, 18), (12, 14, 17, 18)))),
    ]
    for _, _, action in sorted(timeline, key=lambda item: item[:2]):
        action()
    for dx in (0, 3, 1, 2):
        for share in shares[dx]:
            share.wait_recv()
    mine = pl.ds(pl.multiple_of(e * tok_dev, tok_dev), tok_dev)
    total = part[mine, :].astype(f32)
    for d in range(7):
        total = total + from_exp[d].astype(f32)
    residual = (hidden[mine, :].astype(f32) + total).astype(bf16)
    residual_out[...] = residual
    wide = residual.astype(f32)
    inverse = lax.rsqrt(jnp.mean(wide * wide, axis=-1, keepdims=True) + 1e-05)
    ready = (wide * inverse * ffn_gain[...].astype(f32)[None]).astype(bf16)
    chosen = jnp.dot(select[...], ready, preferred_element_type=f32)
    slots[...] = chosen.reshape(slots.shape).astype(bf16)
    moves = [
        pltpu.make_async_remote_copy(
            src_ref=slots.at[to],
            dst_ref=arrived_out.at[e],
            send_sem=to_send.at[d],
            recv_sem=to_recv.at[d],
            device_id=(c, to),
            device_id_type=MESH,
        )
        for d, to in enumerate(peers)
    ]
    for move in moves:
        move.start()
    arrived_out[e] = slots[e]
    for piece in pieces + [now]:
        piece.drain()
    for dx in (0, 3, 1, 2):
        for share in shares[dx]:
            share.wait_send()
    for move in moves:
        move.wait_send()
    for move in moves:
        move.wait_recv()


def mixer(hidden, attn_gain, w_query, w_key, w_value, w_out, prior_keys, prior_values, cosine, sine, ffn_gain, select):
    tokens, width = hidden.shape
    depth, q_cols = w_query.shape
    bf16, f32 = jnp.bfloat16, jnp.float32
    span = 16 * tokens
    count = q_cols // HEAD_DIM * tokens
    vmem = pl.BlockSpec(memory_space=pltpu.VMEM)
    anywhere = pl.BlockSpec(memory_space=pltpu.HBM)
    return pl.pallas_call(
        mixer_kernel,
        out_shape=[
            jax.ShapeDtypeStruct((tokens // 8, width), bf16),
            jax.ShapeDtypeStruct((8, select.shape[0] // 8, width), bf16),
        ],
        in_specs=[vmem, vmem] + [anywhere] * 6 + [vmem] * 4,
        out_specs=[vmem] * 2,
        scratch_shapes=[
            pltpu.VMEM((tokens, width), bf16),
            pltpu.VMEM((16 * depth, 2 * HEAD_DIM), bf16),
            pltpu.VMEM((16 * depth, q_cols), bf16),
            pltpu.VMEM((2 * span, 2 * HEAD_DIM), bf16),
            pltpu.VMEM((w_out.shape[0], width), bf16),
            pltpu.VMEM((count, HEAD_DIM), bf16),
            pltpu.VMEM((count, span + tokens), f32),
            pltpu.VMEM((count, tokens), f32),
            pltpu.VMEM((count, tokens), f32),
            pltpu.VMEM((count, HEAD_DIM), f32),
            pltpu.VMEM((tokens, q_cols), bf16),
            pltpu.VMEM((tokens, width), bf16),
            pltpu.VMEM((7, tokens // 8, width), bf16),
            pltpu.VMEM((8, select.shape[0] // 8, width), bf16),
            pltpu.SemaphoreType.DMA((9, N_TRANSFERS)),
            pltpu.SemaphoreType.DMA((9, N_TRANSFERS)),
            pltpu.SemaphoreType.DMA((6,)),
            pltpu.SemaphoreType.DMA((4, 7)),
            pltpu.SemaphoreType.DMA((4, 7)),
            pltpu.SemaphoreType.DMA((7,)),
            pltpu.SemaphoreType.DMA((7,)),
        ],
        compiler_params=pltpu.CompilerParams(
            collective_id=0, has_side_effects=True, vmem_limit_bytes=60 * 1024 * 1024
        ),
        name="mixer",
    )(hidden, attn_gain, w_query, w_key, w_value, w_out, prior_keys, prior_values, cosine, sine, ffn_gain, select)


def local(
    hidden_in,
    attn_gain,
    w_query,
    w_key,
    w_value,
    w_out,
    prior_keys,
    prior_values,
    stretch_offset,
    ffn_gain,
    w_gate,
    w_up,
    w_down,
    expert_ids,
    gate_weights,
):
    exp_count = lax.axis_size("exp")
    ctx_index = lax.axis_index("ctx")
    exp_index = lax.axis_index("exp")
    local_len, model_width = hidden_in.shape
    tok_dev = local_len // exp_count
    positions = stretch_offset[0] + ctx_index * local_len + jnp.arange(local_len, dtype=jnp.int32)
    half_dim = HEAD_DIM // 2
    frequency = jnp.exp(jnp.arange(half_dim).astype(jnp.float32) * (-2.0 * math.log(1000000.0) / HEAD_DIM))
    angles = positions.astype(jnp.float32)[:, None] * frequency[None, :]
    cosine, sine = jnp.cos(angles), jnp.sin(angles)
    capacity = 4 * tok_dev // exp_count
    device_row = (ctx_index * exp_count + exp_index) * tok_dev
    my_ids = lax.dynamic_slice_in_dim(expert_ids, device_row, tok_dev, 0)
    flat = my_ids.reshape(-1)
    same = flat[:, None] == flat[None, :]
    earlier = jnp.arange(2 * tok_dev)[:, None] < jnp.arange(2 * tok_dev)[None, :]
    place = flat * capacity + jnp.sum(same & earlier, axis=0, dtype=jnp.int32)
    place = place.reshape(tok_dev, 2)
    slot = jnp.arange(exp_count * capacity, dtype=jnp.int32)
    select = ((slot[:, None] == place[None, :, 0]) | (slot[:, None] == place[None, :, 1])).astype(jnp.bfloat16)
    mix = jnp.where(place[:, :1] == slot[None, :], gate_weights[:, :1], 0.0) + jnp.where(
        place[:, 1:] == slot[None, :], gate_weights[:, 1:], 0.0
    )
    residual, arrived = mixer(
        hidden_in,
        attn_gain,
        w_query,
        w_key,
        w_value,
        w_out,
        prior_keys,
        prior_values,
        jnp.concatenate([cosine, cosine], axis=1),
        jnp.concatenate([-sine, sine], axis=1),
        ffn_gain,
        select,
    )
    return experts(arrived.reshape(-1, model_width), w_gate, w_up, w_down, residual, mix)


def solution(mesh):
    in_specs = (
        P("ctx", None),
        P(),
        P("ctx", "exp"),
        P("ctx", "exp"),
        P("ctx", "exp"),
        P("exp", "ctx"),
        P("ctx", "exp"),
        P("ctx", "exp"),
        P(),
        P(),
        P("exp", None, "ctx"),
        P("exp", None, "ctx"),
        P("exp", "ctx", None),
        P(),
        P(("ctx", "exp"), None),
    )
    out_specs = P(("ctx", "exp"), None)
    return jax.shard_map(local, mesh=mesh, in_specs=in_specs, out_specs=out_specs, check_vma=False)
```
